512 devices in a mesh: member: 16 (over z, core), point: 32 (over y, x).
Axes of the slice: x: 4, y: 8, z: 8, core: 2. Of those that a mesh axis runs over, the one named last changes fastest.
Arguments:
- ensemble: float32 [32, 655360], P('member', 'point'), may hold values from -6 to 6
- inputs: bfloat16 [6144, 1024], P('point'), may hold values from -6 to 6
- features: bfloat16 [128, 256], replicated, may hold values from -6 to 6
- query_index: int32 [393216], P('point'), may hold values from 0 to 127
- observed: float32 [393216], P('point'), may hold values from -6 to 6
- perturb: float32 [32, 393216], P('member', 'point'), may hold values from -3 to 3
Outputs:
- theta_next: float32 [32, 655360], P('member', 'point')
- coefficients: float32 [32, 32], replicated
The draws below stay inside these ranges and needn't reach their ends.
All inputs are finite; a program needn't handle non-finite values.
Results may differ from the reference program's by a relative error of at most 0.0003.
Values may be sent and summed in bfloat16 or wider, within the bound.
No kernel may reach another device: no remote copies, remote signals or barrier semaphores. Data moves between devices by JAX's collectives and lax.ppermute only.
A program may use at most 64 MiB of HBM per device.

```python
import jax
import jax.numpy as jnp
from jax import lax

SENSORS = 1024
WIDTH = 256
BASIS = 512
FEATS = 256
NQ = 128
QOBS = 64
SUBSTEPS = 2
MEMBERS = 32
NIN = 6144
NOBS = 393216
PARAMS = 655360


def set_ends(array, own_key, smallest, top_value):
    longest = array.shape.index(max(array.shape))
    spots = []
    for shift in (0, 1):
        where = [jax.random.randint(jax.random.fold_in(own_key, axis), (), 0, length) for axis, length in enumerate(array.shape)]
        where[longest] = (where[longest] + shift) % array.shape[longest]
        spots.append(tuple(where))
    return array.at[spots[0]].set(smallest).at[spots[1]].set(top_value)


def block_scale(stream_key, dims, shards, smallest, top_value):
    def one(dim, parts):
        heights = jax.random.uniform(jax.random.fold_in(jax.random.fold_in(stream_key, 6), dim), (parts,), jnp.float32, smallest / len(shards), top_value / len(shards))
        return jnp.repeat(jnp.exp(heights), dims[dim] // parts).reshape((-1,) + (1,) * (len(dims) - dim - 1))

    factor_of = one(*shards[0])
    for cut in shards[1:]:
        factor_of = factor_of * one(*cut)
    return factor_of


def scatter_about(own_key, shape, deviation, bound, shards=(), kind=jnp.bfloat16):
    factor_of = block_scale(own_key, shape, shards, -0.22, 0.18) if shards else 1.0
    result = jax.random.normal(own_key, shape, jnp.float32) * deviation * factor_of
    return jnp.minimum(jnp.maximum(result, -bound), bound).astype(kind)


def setup_inputs(seed: int = 0) -> dict:
    seeds = jax.random.split(jax.random.key(seed), 7)
    return {
        "ensemble": scatter_about(seeds[0], (MEMBERS, PARAMS), 1.0, 6.0, ((0, 16), (1, 32)), jnp.float32),
        "inputs": scatter_about(seeds[1], (NIN, SENSORS), 1.0, 6.0, ((0, 32),)),
        "features": scatter_about(seeds[2], (NQ, FEATS), 1.0, 6.0),
        "query_index": set_ends(jax.random.randint(seeds[3], (NOBS,), 0, NQ), jax.random.fold_in(seeds[3], 1), 0, NQ - 1).astype(jnp.int32),
        "observed": scatter_about(seeds[4], (NOBS,), 1.0, 6.0, ((0, 32),), jnp.float32),
        "perturb": scatter_about(seeds[5], (MEMBERS, NOBS), 0.5, 3.0, ((0, 16), (1, 32)), jnp.float32),
    }


NOISE_STD = 0.5
RIDGE_SHARE = 0.5

def member_outputs(flat, inputs, features, picks):
    first = SENSORS * WIDTH
    second = first + WIDTH * WIDTH
    third = second + WIDTH * BASIS
    fourth = third + FEATS * WIDTH
    branch_in = flat[:first].reshape(SENSORS, WIDTH)
    branch_mid = flat[first:second].reshape(WIDTH, WIDTH)
    branch_out = flat[second:third].reshape(WIDTH, BASIS)
    trunk_in = flat[third:fourth].reshape(FEATS, WIDTH)
    trunk_out = flat[fourth:].reshape(WIDTH, BASIS)
    hidden = jnp.tanh(jnp.dot(inputs.astype(jnp.float32), branch_in.astype(jnp.float32), preferred_element_type=jnp.float32) * SENSORS ** (-0.5)).astype(jnp.bfloat16)
    hidden = jnp.tanh(jnp.dot(hidden.astype(jnp.float32), branch_mid.astype(jnp.float32), preferred_element_type=jnp.float32) * WIDTH ** (-0.5)).astype(jnp.bfloat16)
    branch = (jnp.dot(hidden.astype(jnp.float32), branch_out.astype(jnp.float32), preferred_element_type=jnp.float32) * WIDTH ** (-0.5)).astype(jnp.bfloat16)
    trunk_hidden = jnp.tanh(jnp.dot(features.astype(jnp.float32), trunk_in.astype(jnp.float32), preferred_element_type=jnp.float32) * FEATS ** (-0.5)).astype(jnp.bfloat16)
    trunk = (jnp.dot(trunk_hidden.astype(jnp.float32), trunk_out.astype(jnp.float32), preferred_element_type=jnp.float32) * WIDTH ** (-0.5)).astype(jnp.bfloat16)
    whole = jnp.dot(branch.astype(jnp.float32), trunk.T.astype(jnp.float32), preferred_element_type=jnp.float32) * BASIS ** (-0.5)
    return jnp.take_along_axis(whole, picks, axis=1).reshape(-1)

def reference(ensemble, inputs, features, query_index, observed, perturb):
    members = ensemble.shape[0]
    picks = query_index.reshape(NIN, QOBS)
    state = ensemble
    coefficients = jnp.zeros((members, members), jnp.float32)
    for repeat in range(SUBSTEPS):
        weights = state.astype(jnp.bfloat16)

        def evaluate(flat):
            return member_outputs(flat, inputs, features, picks)
        preds = lax.map(evaluate, weights).astype(jnp.bfloat16)
        preds = lax.optimization_barrier(preds)
        pred_vals = preds.astype(jnp.float32)
        innov = ((observed[None, :] + perturb - pred_vals) / NOISE_STD).astype(jnp.bfloat16)
        pred_anom = (pred_vals - jnp.mean(pred_vals, axis=0)) / (NOISE_STD * (members - 1) ** 0.5)
        par_anom = (state - jnp.mean(state, axis=0)) / (members - 1) ** 0.5
        gram = jnp.dot(pred_anom, pred_anom.T, precision=lax.Precision.HIGHEST) + jnp.dot(par_anom, par_anom.T, precision=lax.Precision.HIGHEST)
        cross = jnp.dot(pred_anom, innov.astype(jnp.float32).T, precision=lax.Precision.HIGHEST) - jnp.dot(par_anom, state.T, precision=lax.Precision.HIGHEST)
        ridge = RIDGE_SHARE * jnp.trace(gram) / members
        system = gram + ridge * jnp.eye(members, dtype=jnp.float32)
        factor = jnp.linalg.cholesky(system)
        coefficients = jax.scipy.linalg.cho_solve((factor, True), cross)
        state = state + jnp.dot(coefficients.T, par_anom, precision=lax.Precision.HIGHEST)
    return (state, coefficients)
```

```python
import functools

import jax
import jax.numpy as jnp
from jax import lax
from jax.experimental import pallas as pl
from jax.experimental.pallas import tpu as pltpu
from jax.sharding import Mesh, PartitionSpec as P

SENSORS = 1024
WIDTH = 256
BASIS = 512
FEATS = 256
QOBS = 64
SUBSTEPS = 2
MEMBERS = 32
NOISE_STD = 0.5
RIDGE_SHARE = 0.5
ROWS = 40
F32, BF16 = jnp.float32, jnp.bfloat16
HIGHEST = lax.Precision.HIGHEST
VMEM = pl.BlockSpec(memory_space=pltpu.VMEM)
SMEM = pl.BlockSpec(memory_space=pltpu.SMEM)


def mxu(a, b):
    return jnp.dot(a, b, preferred_element_type=F32)


def interleave_matrix():
    r = lax.broadcasted_iota(jnp.int32, (256, 256), 0)
    s = lax.broadcasted_iota(jnp.int32, (256, 256), 1)
    return (s == (r % 2) * 128 + r // 2).astype(F32).astype(BF16)


def evaluate_kernel(w_ref, x_ref, features_ref, out_ref, whole_ref):
    mix = interleave_matrix()

    def narrow(start):
        both = jnp.concatenate([w_ref[0, start : start + 128, :], w_ref[1, start : start + 128, :]], 0)
        return mxu(mix, both).astype(BF16)

    branch_in, branch_mid, branch_out, trunk_in, trunk_out = 0, 512, 640, 896, 1024
    trunk_hidden = jnp.tanh(mxu(features_ref[...], narrow(trunk_in)) * FEATS ** (-0.5)).astype(BF16)
    trunk = [
        (mxu(trunk_hidden, w_ref[c, trunk_out : trunk_out + 256, :]) * WIDTH ** (-0.5)).astype(BF16)
        for c in range(2)
    ]
    total = None
    for i in range(4):
        part = mxu(x_ref[:, 256 * i : 256 * i + 256], narrow(branch_in + 128 * i))
        total = part if total is None else total + part
    hidden = jnp.tanh(total * SENSORS ** (-0.5)).astype(BF16)
    hidden = jnp.tanh(mxu(hidden, narrow(branch_mid)) * WIDTH ** (-0.5)).astype(BF16)
    whole = None
    for c in range(2):
        branch = (mxu(hidden, w_ref[c, branch_out : branch_out + 256, :]) * WIDTH ** (-0.5)).astype(BF16)
        part = lax.dot_general(branch, trunk[c], (((1,), (1,)), ((), ())), preferred_element_type=F32)
        whole = part if whole is None else whole + part
    whole = whole * BASIS ** (-0.5)
    picks = x_ref[:, SENSORS : SENSORS + 128].astype(F32).astype(jnp.int32)
    whole_ref[...] = jnp.take_along_axis(whole, picks, axis=1, mode="promise_in_bounds")
    left = lax.broadcasted_iota(jnp.int32, (8, 128), 1) < QOBS
    for x in range(4):
        for k in range(0, 12, 2):
            first = whole_ref[pl.ds(x * 96 + k, 8, stride=12), :]
            second = whole_ref[pl.ds(x * 96 + k + 1, 8, stride=12), :]
            out_ref[x * 8 : x * 8 + 8, k * QOBS : k * QOBS + 128] = jnp.where(left, first, second)


def evaluate(weights, inputs_ext, features):
    return pl.pallas_call(
        evaluate_kernel,
        out_shape=jax.ShapeDtypeStruct((32, 12 * QOBS), F32),
        in_specs=[VMEM] * 3,
        out_specs=VMEM,
        scratch_shapes=[pltpu.VMEM((384, 128), F32)],
        name="evaluate",
    )(weights, inputs_ext, features).astype(BF16)


def contract_last(a, b):
    return lax.dot_general(a, b, (((1,), (1,)), ((), ())), precision=HIGHEST, preferred_element_type=F32)


def fold(square):
    return jnp.concatenate([square[8 * i : 8 * i + 8, :] for i in range(4)], 1)


def unfold(tile):
    return jnp.concatenate([tile[:, 32 * i : 32 * i + 32] for i in range(4)], 0)


def sums_kernel(first, where_ref, preds_ref, target_ref, state_ref, mix_ref, out_ref):
    r = lax.broadcasted_iota(jnp.int32, (32, 32), 0)
    s = lax.broadcasted_iota(jnp.int32, (32, 32), 1)
    order = (s == (r % 4) * 8 + r // 4).astype(F32).astype(BF16)
    preds = mxu(order, preds_ref[...])
    innov = ((target_ref[...] - preds) / NOISE_STD).astype(BF16).astype(F32)
    anom = (preds - jnp.mean(preds, axis=0, keepdims=True)) / (NOISE_STD * (MEMBERS - 1) ** 0.5)
    gram = contract_last(anom, anom)
    cross = contract_last(anom, innov)
    gram_par = jnp.zeros((32, 32), F32)
    cross_par = jnp.zeros((32, 32), F32)
    for row in range(8):
        state = state_ref[:, row, :]
        if not first:
            state = jnp.dot(mix_ref[...], state, precision=HIGHEST, preferred_element_type=F32)
        par_anom = (state - jnp.mean(state, axis=0, keepdims=True)) / (MEMBERS - 1) ** 0.5
        gram_par += contract_last(par_anom, par_anom)
        cross_par += contract_last(par_anom, state)
    share = where_ref[2].astype(F32)
    out_ref[0:8, :] = fold(gram + share * gram_par)
    out_ref[8:16, :] = fold(cross - share * cross_par)


def member_sums(first, where, preds, target, slab, mix):
    whole = lambda shape: pl.BlockSpec(shape, lambda i, w: (0,) * len(shape))
    return pl.pallas_call(
        functools.partial(sums_kernel, first),
        out_shape=jax.ShapeDtypeStruct((16, 128), F32),
        grid_spec=pltpu.PrefetchScalarGridSpec(
            num_scalar_prefetch=1,
            grid=(1,),
            in_specs=[
                whole((32, 768)),
                whole((32, 768)),
                pl.BlockSpec((32, 8, 256), lambda i, w: (0, w[0], w[1])),
                whole((32, 32)),
            ],
            out_specs=whole((16, 128)),
        ),
        name="member_sums",
    )(where, preds, target, slab, mix)


def solve_kernel(first, parts_ref, mix_ref, coefficients_ref, mix_out_ref):
    both = parts_ref[0]
    for i in range(1, 16):
        both = both + parts_ref[i]
    gram, cross = unfold(both[0:8, :]), unfold(both[8:16, :])
    r = lax.broadcasted_iota(jnp.int32, (32, 32), 0)
    s = lax.broadcasted_iota(jnp.int32, (32, 32), 1)
    eye = (r == s).astype(F32)
    trace = jnp.sum(jnp.sum(gram * eye, axis=1, keepdims=True), axis=0, keepdims=True)
    system = gram + (RIDGE_SHARE / MEMBERS) * trace * eye
    table = jnp.concatenate([system, cross], 1)
    line = lax.broadcasted_iota(jnp.int32, (32, 64), 0)
    for k in range(32):
        row = table[k : k + 1, :] / table[k : k + 1, k : k + 1]
        table = jnp.where(line == k, row, table - table[:, k : k + 1] * row)
    coefficients = table[:, 32:64]
    coefficients_ref[...] = coefficients
    turned = lax.dot_general(
        coefficients, eye, (((0,), (0,)), ((), ())), precision=HIGHEST, preferred_element_type=F32
    )
    centred = turned - jnp.mean(turned, axis=1, keepdims=True)
    step = eye + centred / (MEMBERS - 1) ** 0.5
    if not first:
        step = jnp.dot(step, mix_ref[...], precision=HIGHEST, preferred_element_type=F32)
    mix_out_ref[...] = step


def solve(first, parts, mix):
    square = jax.ShapeDtypeStruct((32, 32), F32)
    return pl.pallas_call(
        functools.partial(solve_kernel, first),
        out_shape=(square, square),
        in_specs=[VMEM] * 2,
        out_specs=(VMEM, VMEM),
        name="solve",
    )(parts, mix)


def combine_kernel(count, where_ref, mix_ref, state_ref, out_ref):
    start = where_ref[0]
    for i in range(count):
        total = None
        for j in range(MEMBERS):
            part = mix_ref[start + i, j] * state_ref[j]
            total = part if total is None else total + part
        out_ref[i] = total.astype(out_ref.dtype)


def combine(count, where, mix, slab, width, dtype):
    return pl.pallas_call(
        functools.partial(combine_kernel, count),
        out_shape=jax.ShapeDtypeStruct((count, ROWS, width), dtype),
        grid_spec=pltpu.PrefetchScalarGridSpec(
            num_scalar_prefetch=1,
            grid=(1,),
            in_specs=[
                pl.BlockSpec(memory_space=pltpu.SMEM),
                pl.BlockSpec((MEMBERS, ROWS, width), lambda i, w: (0, 0, w[1])),
            ],
            out_specs=pl.BlockSpec((count, ROWS, width), lambda i, w: (0, 0, 0)),
        ),
        name="combine",
    )(where, mix, slab)


def exchange(blocks, axes):
    return lax.all_to_all(blocks, axes, 0, 0, tiled=True)


def to_all(block, axes, count):
    return exchange(jnp.broadcast_to(block[None], (count,) + block.shape), axes)


def spread_weights(plane):
    blocks = jnp.broadcast_to(plane[None], (8, 4, ROWS, 256)).reshape(32, ROWS, 256)
    half = exchange(blocks, ("y", "x")).reshape(32 * ROWS, 256)
    return to_all(half, "core", 2)


def local(ensemble, inputs, features, query_index, observed, perturb):
    z, core = lax.axis_index("z"), lax.axis_index("core")
    own = ensemble.reshape(2, ROWS, 512)
    slab = lax.all_gather(own, ("z", "core"), axis=0, tiled=True)
    plane = own.astype(BF16).reshape(2, ROWS, 2, 256).transpose(2, 0, 1, 3)
    plane = exchange(plane, "core").reshape(4, ROWS, 256)
    picks = query_index.reshape(192, QOBS).astype(BF16)
    ext = jnp.concatenate([inputs, picks, picks], 1)
    ext = lax.dynamic_slice_in_dim(ext, core * 96, 96, 0)
    ext = lax.all_gather(ext, "x", axis=0, tiled=True)
    noise = perturb.reshape(2, 2, 8, 768).transpose(2, 1, 0, 3).reshape(16, 2, 768)
    noise = exchange(noise, ("z", "core")).reshape(32, 768)
    place = (core * 8 + z) * 768
    target = lax.dynamic_slice_in_dim(observed, place, 768, 0)[None, :] + noise
    e = z * 2 + core
    shared = jnp.stack([jnp.minimum(e, 9) // 2, e % 2, (e < 10).astype(jnp.int32)])
    mix = jnp.zeros((32, 32), F32)
    for repeat in range(SUBSTEPS):
        first = repeat == 0
        if not first:
            plane = combine(4, jnp.stack([4 * z, core]), mix, slab, 256, BF16)
        weights = spread_weights(plane)
        preds = evaluate(weights, ext, features)
        preds = exchange(preds, ("x", "z"))
        part = member_sums(first, shared, preds, target, slab, mix)
        part = jnp.sum(to_all(part, ("z", "x"), 32), axis=0)
        parts = to_all(part, ("y", "core"), 16)
        coefficients, mix = solve(first, parts, mix)
    theta = combine(2, jnp.stack([2 * e, 0]), mix, slab, 512, F32)
    return (theta.reshape(2, ROWS * 512), coefficients)


def solution(mesh):
    grid = Mesh(mesh.devices.reshape(8, 2, 8, 4), ("z", "core", "y", "x"))
    member, point = ("z", "core"), ("y", "x")
    in_specs = (
        P(member, point),
        P(point, None),
        P(),
        P(point),
        P(point),
        P(member, point),
    )
    out_specs = (P(member, point), P())
    return jax.shard_map(local, mesh=grid, in_specs=in_specs, out_specs=out_specs, check_vma=False)
```

```python
import functools

import jax
import jax.numpy as jnp
from jax import lax
from jax.experimental import pallas as pl
from jax.experimental.pallas import tpu as pltpu
from jax.sharding import Mesh, PartitionSpec as P

SENSORS = 1024
WIDTH = 256
BASIS = 512
FEATS = 256
QOBS = 64
SUBSTEPS = 2
MEMBERS = 32
NOISE_STD = 0.5
RIDGE_SHARE = 0.5
ROWS = 40
NOTES = 24
F32, BF16 = jnp.float32, jnp.bfloat16
HIGHEST = lax.Precision.HIGHEST
VMEM = pl.BlockSpec(memory_space=pltpu.VMEM)
SMEM = pl.BlockSpec(memory_space=pltpu.SMEM)


def mxu(a, b):
    return jnp.dot(a, b, preferred_element_type=F32)


def prepare_kernel(where_ref, ensemble_ref, inputs_ref, picks_ref, observed_ref, perturb_ref, own_ref, plane_ref, ext_ref):
    for i in range(2):
        for e in range(16):
            for part in range(3):
                at = 768 * e + 256 * part
                row, left = 3 * (e // 2) + part, 256 * (e % 2)
                own_ref[i, row : row + 1, left : left + 256] = (
                    observed_ref[0:1, at : at + 256] + perturb_ref[i : i + 1, at : at + 256]
                )
        for row in range(ROWS):
            own_ref[i, NOTES + row : NOTES + row + 1, :] = ensemble_ref[i : i + 1, 512 * row : 512 * row + 512]
        for c in range(2):
            plane_ref[c, i] = own_ref[i, NOTES:, 256 * c : 256 * c + 256].astype(BF16)
    core = where_ref[1]
    ext_ref[:, :SENSORS] = inputs_ref[pl.ds(pl.multiple_of(core * 96, 32), 96), :]
    picks = picks_ref[pl.ds(pl.multiple_of(core * 48, 16), 48), :]
    ext_ref[:48, SENSORS:] = picks.astype(F32).astype(BF16)
    ext_ref[48:, SENSORS:] = jnp.zeros((48, 128), BF16)


def prepare(where, ensemble, inputs, picks, observed, perturb):
    return pl.pallas_call(
        prepare_kernel,
        out_shape=(
            jax.ShapeDtypeStruct((2, NOTES + ROWS, 512), F32),
            jax.ShapeDtypeStruct((2, 2, ROWS, 256), BF16),
            jax.ShapeDtypeStruct((96, SENSORS + 128), BF16),
        ),
        in_specs=[SMEM] + [VMEM] * 5,
        out_specs=(VMEM,) * 3,
        name="prepare",
    )(where, ensemble, inputs, picks, observed, perturb)


def evaluate_kernel(where_ref, own_ref, other_ref, x_ref, features_ref, out_ref, whole_ref, chosen_ref):
    r = lax.broadcasted_iota(jnp.int32, (256, 256), 0)
    s = lax.broadcasted_iota(jnp.int32, (256, 256), 1)
    mix = (s == ((r + where_ref[1]) % 2) * 128 + r // 2).astype(F32).astype(BF16)

    def narrow(start):
        both = jnp.concatenate([own_ref[start : start + 128, :], other_ref[start : start + 128, :]], 0)
        return mxu(mix, both).astype(BF16)

    branch_in, branch_mid, branch_out, trunk_in, trunk_out = 0, 512, 640, 896, 1024
    halves = (own_ref, other_ref)
    trunk_hidden = jnp.tanh(mxu(features_ref[...], narrow(trunk_in)) * FEATS ** (-0.5)).astype(BF16)
    trunk = [
        (mxu(trunk_hidden, half[trunk_out : trunk_out + 256, :]) * WIDTH ** (-0.5)).astype(BF16) for half in halves
    ]
    total = None
    for i in range(4):
        part = mxu(x_ref[:, 256 * i : 256 * i + 256], narrow(branch_in + 128 * i))
        total = part if total is None else total + part
    hidden = jnp.tanh(total * SENSORS ** (-0.5)).astype(BF16)
    hidden = jnp.tanh(mxu(hidden, narrow(branch_mid)) * WIDTH ** (-0.5)).astype(BF16)
    whole = None
    for c, half in enumerate(halves):
        branch = (mxu(hidden, half[branch_out : branch_out + 256, :]) * WIDTH ** (-0.5)).astype(BF16)
        part = lax.dot_general(branch, trunk[c], (((1,), (1,)), ((), ())), preferred_element_type=F32)
        whole = part if whole is None else whole + part
    whole_ref[...] = whole * BASIS ** (-0.5)
    left = lax.broadcasted_iota(jnp.int32, (48, 128), 1) < QOBS
    for x in range(4):
        picks = x_ref[96 * x : 96 * x + 48, SENSORS:].astype(F32).astype(jnp.int32)
        even = whole_ref[pl.ds(96 * x, 48, stride=2), :]
        odd = whole_ref[pl.ds(96 * x + 1, 48, stride=2), :]
        chosen_ref[48 * x : 48 * x + 48, :] = jnp.where(
            left,
            jnp.take_along_axis(even, picks, axis=1, mode="promise_in_bounds"),
            jnp.take_along_axis(odd, picks, axis=1, mode="promise_in_bounds"),
        )
    for j in range(6):
        for x in range(0, 4, 2):
            pair = [chosen_ref[pl.ds(48 * (x + h) + j, 8, stride=6), :] for h in range(2)]
            out_ref[8 * x : 8 * x + 16, 128 * j : 128 * j + 128] = jnp.concatenate(pair, 0).astype(BF16)


def evaluate(where, own, other, inputs_ext, features):
    return pl.pallas_call(
        evaluate_kernel,
        out_shape=jax.ShapeDtypeStruct((32, 12 * QOBS), BF16),
        in_specs=[SMEM] + [VMEM] * 4,
        out_specs=VMEM,
        scratch_shapes=[pltpu.VMEM((384, 128), F32), pltpu.VMEM((192, 128), F32)],
        name="evaluate",
    )(where, own, other, inputs_ext, features)


def fold(square):
    return jnp.concatenate([square[8 * i : 8 * i + 8, :] for i in range(4)], 1)


def unfold(tile):
    return jnp.concatenate([tile[:, 32 * i : 32 * i + 32] for i in range(4)], 0)


def sums_kernel(first, where_ref, preds_ref, target_ref, state_ref, mix_ref, out_ref):
    r = lax.broadcasted_iota(jnp.int32, (32, 32), 0)
    s = lax.broadcasted_iota(jnp.int32, (32, 32), 1)
    order = (s == (r % 4) * 8 + r // 4).astype(F32).astype(BF16)
    preds = mxu(order, preds_ref[...])
    row = where_ref[4]
    target = jnp.concatenate([target_ref[:, row + i, :] for i in range(3)], 1)
    innov = ((target - preds) / NOISE_STD).astype(BF16).astype(F32)
    anom = (preds - jnp.mean(preds, axis=0, keepdims=True)) / (NOISE_STD * (MEMBERS - 1) ** 0.5)
    state = jnp.concatenate([state_ref[:, i, :] for i in range(8)], 1)
    if not first:
        state = jnp.dot(mix_ref[...], state, precision=HIGHEST, preferred_element_type=F32)
    par_anom = (state - jnp.mean(state, axis=0, keepdims=True)) / (MEMBERS - 1) ** 0.5
    share = where_ref[6].astype(F32)
    lhs = jnp.concatenate([anom, par_anom * share], 1)
    rhs = jnp.concatenate([jnp.concatenate([anom, par_anom], 1), jnp.concatenate([innov, -state], 1)], 0)
    both = lax.dot_general(lhs, rhs, (((1,), (1,)), ((), ())), precision=HIGHEST, preferred_element_type=F32)
    packed = jnp.concatenate([fold(both[:, :32]), fold(both[:, 32:])], 0)
    for i in range(32):
        out_ref[i] = packed


def member_sums(first, where, preds, slab, mix):
    whole = lambda shape: pl.BlockSpec(shape, lambda i, w: (0,) * len(shape))
    return pl.pallas_call(
        functools.partial(sums_kernel, first),
        out_shape=jax.ShapeDtypeStruct((32, 16, 128), F32),
        grid_spec=pltpu.PrefetchScalarGridSpec(
            num_scalar_prefetch=1,
            grid=(1,),
            in_specs=[
                whole((32, 768)),
                pl.BlockSpec((32, NOTES, 256), lambda i, w: (0, 0, w[3])),
                pl.BlockSpec((32, 8, 256), lambda i, w: (0, w[5], w[7])),
                whole((32, 32)),
            ],
            out_specs=whole((32, 16, 128)),
        ),
        name="member_sums",
    )(where, preds, slab, slab, mix)


def solve_kernel(last, where_ref, parts_ref, mix_ref, slab_ref, coefficients_ref, mix_out_ref, state_ref):
    both = parts_ref[0]
    for i in range(1, 16):
        both = both + parts_ref[i]
    gram, cross = unfold(both[0:8, :]), unfold(both[8:16, :])
    r = lax.broadcasted_iota(jnp.int32, (32, 32), 0)
    s = lax.broadcasted_iota(jnp.int32, (32, 32), 1)
    eye = (r == s).astype(F32)
    trace = jnp.sum(jnp.sum(gram * eye, axis=1, keepdims=True), axis=0, keepdims=True)
    system = gram + (RIDGE_SHARE / MEMBERS) * trace * eye
    table = jnp.concatenate([system, cross], 1)
    line = lax.broadcasted_iota(jnp.int32, (32, 64), 0)
    for k in range(0, 32, 2):
        upper, lower = table[k : k + 1, :], table[k + 1 : k + 2, :]
        a, b = upper[:, k : k + 1], upper[:, k + 1 : k + 2]
        c, d = lower[:, k : k + 1], lower[:, k + 1 : k + 2]
        inverse = 1.0 / (a * d - b * c)
        new_upper = (d * upper - b * lower) * inverse
        new_lower = (a * lower - c * upper) * inverse
        rest = table - table[:, k : k + 1] * new_upper - table[:, k + 1 : k + 2] * new_lower
        table = jnp.where(line == k, new_upper, jnp.where(line == k + 1, new_lower, rest))
    coefficients = table[:, 32:64]
    coefficients_ref[...] = coefficients
    turned = lax.dot_general(
        coefficients, eye, (((0,), (0,)), ((), ())), precision=HIGHEST, preferred_element_type=F32
    )
    centred = turned - jnp.mean(turned, axis=1, keepdims=True)
    step = eye + centred / (MEMBERS - 1) ** 0.5
    step = jnp.dot(step, mix_ref[...], precision=HIGHEST, preferred_element_type=F32)
    mix_out_ref[...] = step
    count = 2 if last else 4
    rows = mix_out_ref[pl.ds(where_ref[2 if last else 0], count), :]
    left = pl.multiple_of(where_ref[1] * 256, 256)
    for i in range(count):
        total = None
        for j in range(MEMBERS):
            part = slab_ref[j, NOTES:, :] if last else slab_ref[j, NOTES:, pl.ds(left, 256)]
            part = rows[i : i + 1, j : j + 1] * part
            total = part if total is None else total + part
        if last:
            for row in range(ROWS):
                state_ref[i : i + 1, 512 * row : 512 * row + 512] = total[row : row + 1, :]
        else:
            for y in range(8):
                state_ref[y, i] = total.astype(BF16)


def solve(last, where, parts, mix, slab):
    square = jax.ShapeDtypeStruct((32, 32), F32)
    state = (
        jax.ShapeDtypeStruct((2, ROWS * 512), F32) if last else jax.ShapeDtypeStruct((8, 4, ROWS, 256), BF16)
    )
    return pl.pallas_call(
        functools.partial(solve_kernel, last),
        out_shape=(square, square, state),
        in_specs=[SMEM] + [VMEM] * 3,
        out_specs=(VMEM,) * 3,
        name="solve",
    )(where, parts, mix, slab)


def exchange(blocks, axes):
    return lax.all_to_all(blocks, axes, 0, 0, tiled=True)


def local(ensemble, inputs, features, query_index, observed, perturb):
    z, core = lax.axis_index("z"), lax.axis_index("core")
    e, block = z * 2 + core, core * 8 + z
    where = jnp.stack(
        [4 * z, core, 2 * e, block % 2, 3 * (block // 2), 3 + jnp.minimum(e, 9) // 2, (e < 10).astype(jnp.int32), e % 2]
    )
    own, plane, ext = prepare(
        where, ensemble, inputs, query_index.reshape(96, 128), observed.reshape(1, -1), perturb
    )
    slab = lax.all_gather(own, ("z", "core"), axis=0, tiled=True)
    plane = exchange(plane, "core").reshape(4, ROWS, 256)
    plane = jnp.broadcast_to(plane[None], (8, 4, ROWS, 256))
    ext = lax.all_gather(ext, "x", axis=0, tiled=True)
    mix = jnp.eye(MEMBERS, dtype=F32)
    for repeat in range(SUBSTEPS):
        half = exchange(plane.reshape(32, ROWS, 256), ("y", "x")).reshape(32 * ROWS, 256)
        other = lax.ppermute(half, "core", [(0, 1), (1, 0)])
        preds = evaluate(where, half, other, ext, features)
        preds = exchange(preds, ("x", "z"))
        parts = exchange(member_sums(repeat == 0, where, preds, slab, mix), ("z", "x"))
        part = jnp.sum(parts, axis=0)
        parts = exchange(jnp.broadcast_to(part[None], (16, 16, 128)), ("y", "core"))
        coefficients, mix, plane = solve(repeat == SUBSTEPS - 1, where, parts, mix, slab)
    return (plane, coefficients)


def solution(mesh):
    grid = Mesh(mesh.devices.reshape(8, 2, 8, 4), ("z", "core", "y", "x"))
    member, point = ("z", "core"), ("y", "x")
    in_specs = (
        P(member, point),
        P(point, None),
        P(),
        P(point),
        P(point),
        P(member, point),
    )
    out_specs = (P(member, point), P())
    return jax.shard_map(local, mesh=grid, in_specs=in_specs, out_specs=out_specs, check_vma=False)
```

```python
import functools

import jax
import jax.numpy as jnp
from jax import lax
from jax.experimental import pallas as pl
from jax.experimental.pallas import tpu as pltpu
from jax.sharding import Mesh, PartitionSpec as P

SENSORS = 1024
WIDTH = 256
BASIS = 512
FEATS = 256
QOBS = 64
SUBSTEPS = 2
MEMBERS = 32
NOISE_STD = 0.5
RIDGE_SHARE = 0.5
ROWS = 40
NOTES = 24
F32, BF16 = jnp.float32, jnp.bfloat16
HIGHEST = lax.Precision.HIGHEST
VMEM = pl.BlockSpec(memory_space=pltpu.VMEM)
SMEM = pl.BlockSpec(memory_space=pltpu.SMEM)


def in_vmem(x):
    return pltpu.with_memory_space_constraint(x, pltpu.VMEM)


def mxu(a, b):
    return jnp.dot(a, b, preferred_element_type=F32)


def prepare_kernel(where_ref, ensemble_ref, inputs_ref, picks_ref, observed_ref, perturb_ref, own_ref, plane_ref, ext_ref, mix_ref):
    for i in range(2):
        for e in range(16):
            for part in range(3):
                at = 768 * e + 256 * part
                row, left = 3 * (e // 2) + part, 256 * (e % 2)
                own_ref[i, row : row + 1, left : left + 256] = (
                    observed_ref[0:1, at : at + 256] + perturb_ref[i : i + 1, at : at + 256]
                )
        for row in range(ROWS):
            own_ref[i, NOTES + row : NOTES + row + 1, :] = ensemble_ref[i : i + 1, 512 * row : 512 * row + 512]
        for c in range(2):
            plane_ref[c, i] = own_ref[i, NOTES:, 256 * c : 256 * c + 256].astype(BF16)
    r = lax.broadcasted_iota(jnp.int32, (32, 32), 0)
    s = lax.broadcasted_iota(jnp.int32, (32, 32), 1)
    mix_ref[...] = (r == s).astype(F32)
    core = where_ref[1]
    ext_ref[:, :SENSORS] = inputs_ref[pl.ds(pl.multiple_of(core * 96, 32), 96), :]
    picks = picks_ref[pl.ds(pl.multiple_of(core * 48, 16), 48), :]
    ext_ref[:48, SENSORS:] = picks.astype(F32).astype(BF16)
    ext_ref[48:, SENSORS:] = jnp.zeros((48, 128), BF16)


def prepare(where, ensemble, inputs, picks, observed, perturb):
    return pl.pallas_call(
        prepare_kernel,
        out_shape=(
            jax.ShapeDtypeStruct((2, NOTES + ROWS, 512), F32),
            jax.ShapeDtypeStruct((2, 2, ROWS, 256), BF16),
            jax.ShapeDtypeStruct((96, SENSORS + 128), BF16),
            jax.ShapeDtypeStruct((32, 32), F32),
        ),
        in_specs=[SMEM] + [VMEM] * 5,
        out_specs=(VMEM,) * 4,
        name="prepare",
    )(where, ensemble, inputs, picks, observed, perturb)


def evaluate_kernel(where_ref, own_ref, other_ref, x_ref, features_ref, out_ref, whole_ref, chosen_ref):
    r = lax.broadcasted_iota(jnp.int32, (256, 256), 0)
    s = lax.broadcasted_iota(jnp.int32, (256, 256), 1)
    mix = (s == ((r + where_ref[1]) % 2) * 128 + r // 2).astype(F32).astype(BF16)

    def narrow(start):
        both = jnp.concatenate([own_ref[start : start + 128, :], other_ref[start : start + 128, :]], 0)
        return mxu(mix, both).astype(BF16)

    branch_in, branch_mid, branch_out, trunk_in, trunk_out = 0, 512, 640, 896, 1024
    halves = (own_ref, other_ref)
    trunk_hidden = jnp.tanh(mxu(features_ref[...], narrow(trunk_in)) * FEATS ** (-0.5)).astype(BF16)
    trunk = [
        (mxu(trunk_hidden, half[trunk_out : trunk_out + 256, :]) * WIDTH ** (-0.5)).astype(BF16) for half in halves
    ]
    total = None
    for i in range(4):
        part = mxu(x_ref[:, 256 * i : 256 * i + 256], narrow(branch_in + 128 * i))
        total = part if total is None else total + part
    hidden = jnp.tanh(total * SENSORS ** (-0.5)).astype(BF16)
    hidden = jnp.tanh(mxu(hidden, narrow(branch_mid)) * WIDTH ** (-0.5)).astype(BF16)
    whole = None
    for c, half in enumerate(halves):
        branch = (mxu(hidden, half[branch_out : branch_out + 256, :]) * WIDTH ** (-0.5)).astype(BF16)
        part = lax.dot_general(branch, trunk[c], (((1,), (1,)), ((), ())), preferred_element_type=F32)
        whole = part if whole is None else whole + part
    whole_ref[...] = whole * BASIS ** (-0.5)
    left = lax.broadcasted_iota(jnp.int32, (48, 128), 1) < QOBS
    for x in range(4):
        picks = x_ref[96 * x : 96 * x + 48, SENSORS:].astype(F32).astype(jnp.int32)
        even = whole_ref[pl.ds(96 * x, 48, stride=2), :]
        odd = whole_ref[pl.ds(96 * x + 1, 48, stride=2), :]
        chosen_ref[48 * x : 48 * x + 48, :] = jnp.where(
            left,
            jnp.take_along_axis(even, picks, axis=1, mode="promise_in_bounds"),
            jnp.take_along_axis(odd, picks, axis=1, mode="promise_in_bounds"),
        )
    for i in range(32):
        out_ref[i] = chosen_ref[6 * i : 6 * i + 6, :].astype(BF16)


def evaluate(where, own, other, inputs_ext, features):
    return pl.pallas_call(
        evaluate_kernel,
        out_shape=jax.ShapeDtypeStruct((32, 6, 128), BF16),
        in_specs=[SMEM] + [VMEM] * 4,
        out_specs=VMEM,
        scratch_shapes=[pltpu.VMEM((384, 128), F32), pltpu.VMEM((192, 128), F32)],
        name="evaluate",
    )(where, in_vmem(own), in_vmem(other), inputs_ext, features)


def split(x):
    high = x.astype(BF16)
    rest = x - high.astype(F32)
    middle = rest.astype(BF16)
    return high, middle, (rest - middle.astype(F32)).astype(BF16)


def sums_kernel(first, where_ref, preds_ref, target_ref, state_ref, mix_ref, out_ref, preds_f32_ref):
    r = lax.broadcasted_iota(jnp.int32, (32, 32), 0)
    s = lax.broadcasted_iota(jnp.int32, (32, 32), 1)
    order = (s == (r % 4) * 8 + r // 4).astype(F32).astype(BF16)
    preds_f32_ref[...] = preds_ref[...].astype(F32)
    preds = jnp.concatenate([preds_f32_ref[:, i, :] for i in range(6)], 1)
    preds = mxu(order, preds.astype(BF16))
    row = where_ref[4]
    target = jnp.concatenate([target_ref[:, row + i, :] for i in range(3)], 1)
    innov = ((target - preds) / NOISE_STD).astype(BF16)
    anom = (preds - jnp.mean(preds, axis=0, keepdims=True)) / (NOISE_STD * (MEMBERS - 1) ** 0.5)
    state = jnp.concatenate([state_ref[:, i, :] for i in range(8)], 1)
    if not first:
        state = jnp.dot(mix_ref[...], state, precision=HIGHEST, preferred_element_type=F32)
    share = where_ref[6].astype(F32)
    par_anom = (state - jnp.mean(state, axis=0, keepdims=True)) * (share / (MEMBERS - 1) ** 0.5)
    lefts = [jnp.concatenate(pair, 1) for pair in zip(split(anom), split(par_anom))]
    nothing = jnp.zeros_like(innov)
    rights = [jnp.concatenate(pair, 1) for pair in zip((innov, nothing, nothing), split(-state))]
    lhs = jnp.concatenate(lefts, 0)
    rhs = jnp.concatenate([term for pair in zip(lefts, rights) for term in pair], 0)
    terms = lax.dot_general(lhs, rhs, (((1,), (1,)), ((), ())), preferred_element_type=F32)
    terms = terms[0:32] + terms[32:64] + terms[64:96]
    both = terms[:, 0:64] + terms[:, 64:128] + terms[:, 128:192]
    packed = jnp.concatenate([both[0:16], both[16:32]], 1)
    for i in range(32):
        out_ref[i] = packed


def member_sums(first, where, preds, slab, mix):
    whole = lambda shape: pl.BlockSpec(shape, lambda i, w: (0,) * len(shape))
    return pl.pallas_call(
        functools.partial(sums_kernel, first),
        out_shape=jax.ShapeDtypeStruct((32, 16, 128), F32),
        grid_spec=pltpu.PrefetchScalarGridSpec(
            num_scalar_prefetch=1,
            grid=(1,),
            in_specs=[
                whole((32, 6, 128)),
                pl.BlockSpec((32, NOTES, 256), lambda i, w: (0, 0, w[3])),
                pl.BlockSpec((32, 8, 256), lambda i, w: (0, w[5], w[7])),
                whole((32, 32)),
            ],
            out_specs=whole((32, 16, 128)),
            scratch_shapes=[pltpu.VMEM((32, 6, 128), F32)],
        ),
        name="member_sums",
    )(where, in_vmem(preds), slab, slab, mix)


def solve_kernel(last, where_ref, parts_ref, mix_ref, slab_ref, coefficients_ref, mix_out_ref, state_ref, held_ref, sem):
    if last:
        wanted = slab_ref.at[:, pl.ds(NOTES, ROWS), :]
    else:
        wanted = slab_ref.at[:, pl.ds(NOTES, ROWS), pl.ds(pl.multiple_of(where_ref[1] * 256, 256), 256)]
    fetch = pltpu.make_async_copy(wanted, held_ref, sem)
    fetch.start()
    both = parts_ref[0]
    for i in range(1, 16):
        both = both + parts_ref[i]
    gram = jnp.concatenate([both[:, 0:32], both[:, 64:96]], 0)
    cross = jnp.concatenate([both[:, 32:64], both[:, 96:128]], 0)
    r = lax.broadcasted_iota(jnp.int32, (32, 32), 0)
    s = lax.broadcasted_iota(jnp.int32, (32, 32), 1)
    eye = (r == s).astype(F32)
    trace = jnp.sum(jnp.sum(gram * eye, axis=1, keepdims=True), axis=0, keepdims=True)
    system = gram + (RIDGE_SHARE / MEMBERS) * trace * eye
    table = jnp.concatenate([system, cross], 1)
    line = lax.broadcasted_iota(jnp.int32, (32, 64), 0)
    for k in range(0, 32, 2):
        first = jnp.broadcast_to(table[:, k : k + 1], (32, 64))
        second = jnp.broadcast_to(table[:, k + 1 : k + 2], (32, 64))
        upper, lower = table[k : k + 1, :], table[k + 1 : k + 2, :]
        a, b, c, d = first[k : k + 1], second[k : k + 1], first[k + 1 : k + 2], second[k + 1 : k + 2]
        inverse = 1.0 / (a * d - b * c)
        new_upper = (d * upper - b * lower) * inverse
        new_lower = (a * lower - c * upper) * inverse
        rest = table - first * new_upper - second * new_lower
        table = jnp.where(line == k, new_upper, jnp.where(line == k + 1, new_lower, rest))
    coefficients = table[:, 32:64]
    coefficients_ref[...] = coefficients
    turned = lax.dot_general(
        coefficients, eye, (((0,), (0,)), ((), ())), precision=HIGHEST, preferred_element_type=F32
    )
    centred = turned - jnp.mean(turned, axis=1, keepdims=True)
    step = eye + centred / (MEMBERS - 1) ** 0.5
    if last:
        step = jnp.dot(step, mix_ref[...], precision=HIGHEST, preferred_element_type=F32)
    mix_out_ref[...] = step
    count = 2 if last else 4
    rows = mix_out_ref[pl.ds(where_ref[2 if last else 0], count), :]
    fetch.wait()
    for i in range(count):
        total = None
        for j in range(MEMBERS):
            part = rows[i : i + 1, j : j + 1] * held_ref[j]
            total = part if total is None else total + part
        if last:
            for row in range(ROWS):
                state_ref[i : i + 1, 512 * row : 512 * row + 512] = total[row : row + 1, :]
        else:
            for y in range(8):
                state_ref[y, i] = total.astype(BF16)


def solve(last, where, parts, mix, slab):
    square = jax.ShapeDtypeStruct((32, 32), F32)
    state = (
        jax.ShapeDtypeStruct((2, ROWS * 512), F32) if last else jax.ShapeDtypeStruct((8, 4, ROWS, 256), BF16)
    )
    return pl.pallas_call(
        functools.partial(solve_kernel, last),
        out_shape=(square, square, state),
        in_specs=[SMEM] + [VMEM] * 2 + [pl.BlockSpec(memory_space=pl.ANY)],
        out_specs=(VMEM,) * 3,
        scratch_shapes=[pltpu.VMEM((MEMBERS, ROWS, 512 if last else 256), F32), pltpu.SemaphoreType.DMA],
        name="solve",
    )(where, in_vmem(parts), mix, slab)


def exchange(blocks, axes):
    return lax.all_to_all(blocks, axes, 0, 0, tiled=True)


def local(ensemble, inputs, features, query_index, observed, perturb):
    z, core = lax.axis_index("z"), lax.axis_index("core")
    e, block = z * 2 + core, core * 8 + z
    where = jnp.stack(
        [4 * z, core, 2 * e, block % 2, 3 * (block // 2), 3 + jnp.minimum(e, 9) // 2, (e < 10).astype(jnp.int32), e % 2]
    )
    own, plane, ext, mix = prepare(
        where, ensemble, inputs, query_index.reshape(96, 128), observed.reshape(1, -1), perturb
    )
    slab = lax.all_gather(own, ("z", "core"), axis=0, tiled=True)
    plane = exchange(plane, "core").reshape(4, ROWS, 256)
    plane = jnp.broadcast_to(plane[None], (8, 4, ROWS, 256))
    ext = lax.all_gather(ext, "x", axis=0, tiled=True)
    for repeat in range(SUBSTEPS):
        half = exchange(plane.reshape(32, ROWS, 256), ("y", "x")).reshape(32 * ROWS, 256)
        half, ext = lax.optimization_barrier((half, ext))
        other = lax.ppermute(half, "core", [(0, 1), (1, 0)])
        preds = evaluate(where, half, other, ext, features)
        preds = exchange(preds, ("x", "z"))
        parts = exchange(member_sums(repeat == 0, where, preds, slab, mix), ("z", "x"))
        part = jnp.sum(parts, axis=0)
        parts = exchange(jnp.broadcast_to(part[None], (16, 16, 128)), ("y", "core"))
        coefficients, mix, plane = solve(repeat == SUBSTEPS - 1, where, parts, mix, slab)
    return (plane, coefficients)


def solution(mesh):
    grid = Mesh(mesh.devices.reshape(8, 2, 8, 4), ("z", "core", "y", "x"))
    member, point = ("z", "core"), ("y", "x")
    in_specs = (
        P(member, point),
        P(point, None),
        P(),
        P(point),
        P(point),
        P(member, point),
    )
    out_specs = (P(member, point), P())
    return jax.shard_map(local, mesh=grid, in_specs=in_specs, out_specs=out_specs, check_vma=False)
```

```python
import functools

import jax
import jax.numpy as jnp
from jax import lax
from jax.experimental import pallas as pl
from jax.experimental.pallas import tpu as pltpu
from jax.sharding import Mesh, PartitionSpec as P

SENSORS = 1024
WIDTH = 256
BASIS = 512
FEATS = 256
QOBS = 64
SUBSTEPS = 2
MEMBERS = 32
NOISE_STD = 0.5
RIDGE_SHARE = 0.5
ROWS = 40
NOTES = 32
F32, BF16 = jnp.float32, jnp.bfloat16
HIGHEST = lax.Precision.HIGHEST
VMEM = pl.BlockSpec(memory_space=pltpu.VMEM)
SMEM = pl.BlockSpec(memory_space=pltpu.SMEM)


def in_vmem(x):
    return pltpu.with_memory_space_constraint(x, pltpu.VMEM)


def mxu(a, b):
    return jnp.dot(a, b, preferred_element_type=F32)


def prepare_kernel(where_ref, ensemble_ref, inputs_ref, picks_ref, observed_ref, perturb_ref, own_ref, keep_ref, give_ref, ext_ref):
    core = where_ref[1]
    for i in range(2):
        for e in range(16):
            for part in range(6):
                at = 768 * e + 128 * part
                row, left = 8 * (e // 4) + part, 128 * (e % 4)
                own_ref[i, row : row + 1, left : left + 128] = (
                    observed_ref[0:1, at : at + 128] + perturb_ref[i : i + 1, at : at + 128]
                )
            own_ref[i, 8 * (e // 4) + 6 : 8 * (e // 4) + 8, 128 * (e % 4) : 128 * (e % 4) + 128] = jnp.zeros((2, 128), F32)
        for row in range(ROWS):
            own_ref[i, NOTES + row : NOTES + row + 1, :] = ensemble_ref[i : i + 1, 512 * row : 512 * row + 512]
        keep_ref[i] = own_ref[i, NOTES:, pl.ds(pl.multiple_of(core * 256, 256), 256)].astype(BF16)
        give_ref[i] = own_ref[i, NOTES:, pl.ds(pl.multiple_of((1 - core) * 256, 256), 256)].astype(BF16)
    ext_ref[:, :SENSORS] = inputs_ref[pl.ds(pl.multiple_of(core * 96, 32), 96), :]
    picks = picks_ref[pl.ds(pl.multiple_of(core * 48, 16), 48), :]
    ext_ref[:48, SENSORS:] = picks.astype(F32).astype(BF16)
    ext_ref[48:, SENSORS:] = jnp.zeros((48, 128), BF16)


def prepare(where, ensemble, inputs, picks, observed, perturb):
    return pl.pallas_call(
        prepare_kernel,
        out_shape=(
            jax.ShapeDtypeStruct((2, NOTES + ROWS, 512), F32),
            pltpu.VMEM((2, ROWS, 256), BF16),
            pltpu.VMEM((2, ROWS, 256), BF16),
            pltpu.VMEM((96, SENSORS + 128), BF16),
        ),
        in_specs=[SMEM] + [VMEM] * 5,
        out_specs=(VMEM,) * 4,
        name="prepare",
    )(where, ensemble, inputs, picks, observed, perturb)


def evaluate_kernel(where_ref, own_ref, other_ref, x_ref, features_ref, out_ref, whole_ref, chosen_ref):
    r = lax.broadcasted_iota(jnp.int32, (256, 256), 0)
    s = lax.broadcasted_iota(jnp.int32, (256, 256), 1)
    mix = (s == ((r + where_ref[1]) % 2) * 128 + r // 2).astype(F32).astype(BF16)

    def narrow(start):
        both = jnp.concatenate([own_ref[start : start + 128, :], other_ref[start : start + 128, :]], 0)
        return mxu(mix, both).astype(BF16)

    branch_in, branch_mid, branch_out, trunk_in, trunk_out = 0, 512, 640, 896, 1024
    halves = (own_ref, other_ref)
    trunk_hidden = jnp.tanh(mxu(features_ref[...], narrow(trunk_in)) * FEATS ** (-0.5)).astype(BF16)
    trunk = [
        (mxu(trunk_hidden, half[trunk_out : trunk_out + 256, :]) * WIDTH ** (-0.5)).astype(BF16) for half in halves
    ]
    total = None
    for i in range(4):
        part = mxu(x_ref[:, 256 * i : 256 * i + 256], narrow(branch_in + 128 * i))
        total = part if total is None else total + part
    hidden = jnp.tanh(total * SENSORS ** (-0.5)).astype(BF16)
    hidden = jnp.tanh(mxu(hidden, narrow(branch_mid)) * WIDTH ** (-0.5)).astype(BF16)
    whole = None
    for c, half in enumerate(halves):
        branch = (mxu(hidden, half[branch_out : branch_out + 256, :]) * WIDTH ** (-0.5)).astype(BF16)
        part = lax.dot_general(branch, trunk[c], (((1,), (1,)), ((), ())), preferred_element_type=F32)
        whole = part if whole is None else whole + part
    whole_ref[...] = whole * BASIS ** (-0.5)
    left = lax.broadcasted_iota(jnp.int32, (48, 128), 1) < QOBS
    for x in range(4):
        picks = x_ref[96 * x : 96 * x + 48, SENSORS:].astype(F32).astype(jnp.int32)
        even = whole_ref[pl.ds(96 * x, 48, stride=2), :]
        odd = whole_ref[pl.ds(96 * x + 1, 48, stride=2), :]
        chosen_ref[48 * x : 48 * x + 48, :] = jnp.where(
            left,
            jnp.take_along_axis(even, picks, axis=1, mode="promise_in_bounds"),
            jnp.take_along_axis(odd, picks, axis=1, mode="promise_in_bounds"),
        )
    for i in range(32):
        out_ref[i] = chosen_ref[6 * i : 6 * i + 6, :].astype(BF16)


def evaluate(where, own, other, inputs_ext, features):
    return pl.pallas_call(
        evaluate_kernel,
        out_shape=pltpu.VMEM((32, 6, 128), BF16),
        in_specs=[SMEM] + [VMEM] * 4,
        out_specs=VMEM,
        scratch_shapes=[pltpu.VMEM((384, 128), F32), pltpu.VMEM((192, 128), F32)],
        name="evaluate",
    )(where, in_vmem(own), in_vmem(other), in_vmem(inputs_ext), features)


def split(x):
    high = x.astype(BF16)
    rest = x - high.astype(F32)
    middle = rest.astype(BF16)
    return high, middle, (rest - middle.astype(F32)).astype(BF16)


def sums_kernel(where_ref, preds_ref, target_ref, state_ref, *rest):
    *mix_ref, out_ref, preds_f32_ref = rest
    r = lax.broadcasted_iota(jnp.int32, (32, 32), 0)
    s = lax.broadcasted_iota(jnp.int32, (32, 32), 1)
    order = (s == (r % 4) * 8 + r // 4).astype(F32).astype(BF16)
    preds_f32_ref[...] = preds_ref[...].astype(F32)
    preds = jnp.concatenate([preds_f32_ref[:, i, :] for i in range(6)], 1)
    preds = mxu(order, preds.astype(BF16))
    target = jnp.concatenate([target_ref[:, i, :] for i in range(6)], 1)
    innov = ((target - preds) / NOISE_STD).astype(BF16)
    anom = (preds - jnp.mean(preds, axis=0, keepdims=True)) / (NOISE_STD * (MEMBERS - 1) ** 0.5)
    state = jnp.concatenate([state_ref[:, i, :] for i in range(8)], 1)
    if mix_ref:
        state = jnp.dot(mix_ref[0][...], state, precision=HIGHEST, preferred_element_type=F32)
    share = where_ref[6].astype(F32)
    par_anom = (state - jnp.mean(state, axis=0, keepdims=True)) * (share / (MEMBERS - 1) ** 0.5)
    lefts = [jnp.concatenate(pair, 1) for pair in zip(split(anom), split(par_anom))]
    nothing = jnp.zeros_like(innov)
    rights = [jnp.concatenate(pair, 1) for pair in zip((innov, nothing, nothing), split(-state))]
    lhs = jnp.concatenate(lefts, 0)
    rhs = jnp.concatenate([term for pair in zip(lefts, rights) for term in pair], 0)
    terms = lax.dot_general(lhs, rhs, (((1,), (1,)), ((), ())), preferred_element_type=F32)
    terms = terms[0:32] + terms[32:64] + terms[64:96]
    both = terms[:, 0:64] + terms[:, 64:128] + terms[:, 128:192]
    packed = jnp.concatenate([both[0:16], both[16:32]], 1)
    for i in range(32):
        out_ref[i] = packed


def member_sums(where, preds, slab, *mix):
    whole = lambda shape: pl.BlockSpec(shape, lambda i, w: (0,) * len(shape))
    return pl.pallas_call(
        sums_kernel,
        out_shape=pltpu.VMEM((32, 16, 128), F32),
        grid_spec=pltpu.PrefetchScalarGridSpec(
            num_scalar_prefetch=1,
            grid=(1,),
            in_specs=[
                whole((32, 6, 128)),
                pl.BlockSpec((32, 8, 128), lambda i, w: (0, w[3], w[4])),
                pl.BlockSpec((32, 8, 256), lambda i, w: (0, w[5], w[7])),
            ]
            + [whole((32, 32)) for _ in mix],
            out_specs=whole((32, 16, 128)),
            scratch_shapes=[pltpu.VMEM((32, 6, 128), F32)],
        ),
        name="member_sums",
    )(where, in_vmem(preds), slab, slab, *mix)


def solve_kernel(last, where_ref, parts_ref, slab_ref, *rest):
    *mix_ref, given_ref, state_ref, held_ref, step_ref, sem = rest
    if last:
        wanted = slab_ref.at[:, pl.ds(NOTES, ROWS), :]
    else:
        wanted = slab_ref.at[:, pl.ds(NOTES, ROWS), pl.ds(pl.multiple_of(where_ref[1] * 256, 256), 256)]
    fetch = pltpu.make_async_copy(wanted, held_ref, sem)
    fetch.start()
    both = parts_ref[0]
    for i in range(1, 16):
        both = both + parts_ref[i]
    gram = jnp.concatenate([both[:, 0:32], both[:, 64:96]], 0)
    cross = jnp.concatenate([both[:, 32:64], both[:, 96:128]], 0)
    r = lax.broadcasted_iota(jnp.int32, (32, 32), 0)
    s = lax.broadcasted_iota(jnp.int32, (32, 32), 1)
    eye = (r == s).astype(F32)
    trace = jnp.sum(jnp.sum(gram * eye, axis=1, keepdims=True), axis=0, keepdims=True)
    system = gram + (RIDGE_SHARE / MEMBERS) * trace * eye
    table = jnp.concatenate([system, cross], 1)
    line = lax.broadcasted_iota(jnp.int32, (32, 64), 0)
    for k in range(0, 32, 2):
        first = jnp.broadcast_to(table[:, k : k + 1], (32, 64))
        second = jnp.broadcast_to(table[:, k + 1 : k + 2], (32, 64))
        upper, lower = table[k : k + 1, :], table[k + 1 : k + 2, :]
        a, b, c, d = first[k : k + 1], second[k : k + 1], first[k + 1 : k + 2], second[k + 1 : k + 2]
        inverse = 1.0 / (a * d - b * c)
        new_upper = (d * upper - b * lower) * inverse
        new_lower = (a * lower - c * upper) * inverse
        rest = table - first * new_upper - second * new_lower
        table = jnp.where(line == k, new_upper, jnp.where(line == k + 1, new_lower, rest))
    coefficients = table[:, 32:64]
    turned = lax.dot_general(
        coefficients, eye, (((0,), (0,)), ((), ())), precision=HIGHEST, preferred_element_type=F32
    )
    centred = turned - jnp.mean(turned, axis=1, keepdims=True)
    step = eye + centred / (MEMBERS - 1) ** 0.5
    if mix_ref:
        step = jnp.dot(step, mix_ref[0][...], precision=HIGHEST, preferred_element_type=F32)
    step_ref[...] = step
    given_ref[...] = coefficients if last else step
    count = 2 if last else 4
    rows = step_ref[pl.ds(where_ref[2 if last else 0], count), :]
    fetch.wait()
    for i in range(count):
        total = None
        for j in range(MEMBERS):
            part = rows[i : i + 1, j : j + 1] * held_ref[j]
            total = part if total is None else total + part
        if last:
            for row in range(ROWS):
                state_ref[i : i + 1, 512 * row : 512 * row + 512] = total[row : row + 1, :]
        else:
            for y in range(8):
                state_ref[y, i] = total.astype(BF16)


def solve(last, where, parts, slab, *mix):
    if last:
        outs = jax.ShapeDtypeStruct((32, 32), F32), jax.ShapeDtypeStruct((2, ROWS * 512), F32)
    else:
        outs = pltpu.VMEM((32, 32), F32), pltpu.VMEM((8, 4, ROWS, 256), BF16)
    return pl.pallas_call(
        functools.partial(solve_kernel, last),
        out_shape=outs,
        in_specs=[SMEM, VMEM, pl.BlockSpec(memory_space=pl.ANY)] + [VMEM for _ in mix],
        out_specs=(VMEM,) * 2,
        scratch_shapes=[
            pltpu.VMEM((MEMBERS, ROWS, 512 if last else 256), F32),
            pltpu.VMEM((32, 32), F32),
            pltpu.SemaphoreType.DMA,
        ],
        name="solve",
    )(where, in_vmem(parts), slab, *mix)


def exchange(blocks, axes):
    return lax.all_to_all(blocks, axes, 0, 0, tiled=True)


def swap(block):
    return lax.ppermute(block, "core", [(0, 1), (1, 0)])


def local(ensemble, inputs, features, query_index, observed, perturb):
    z, core = lax.axis_index("z"), lax.axis_index("core")
    e, block = z * 2 + core, core * 8 + z
    where = jnp.stack(
        [4 * z, core, 2 * e, block // 4, block % 4, 4 + jnp.minimum(e, 9) // 2, (e < 10).astype(jnp.int32), e % 2]
    )
    own, keep, give, ext = prepare(
        where, ensemble, inputs, query_index.reshape(96, 128), observed.reshape(1, -1), perturb
    )
    slab = lax.all_gather(own, ("z", "core"), axis=0, tiled=True)
    taken = swap(give)
    plane = jnp.where(core == 0, jnp.concatenate([keep, taken]), jnp.concatenate([taken, keep]))
    plane = jnp.broadcast_to(plane[None], (8, 4, ROWS, 256))
    ext = lax.all_gather(ext, "x", axis=0, tiled=True)
    mix = []
    for repeat in range(SUBSTEPS):
        half = exchange(plane.reshape(32, ROWS, 256), ("y", "x")).reshape(32 * ROWS, 256)
        half, ext = lax.optimization_barrier((half, ext))
        other = swap(half)
        preds = evaluate(where, half, other, ext, features)
        preds = exchange(preds, ("x", "z"))
        parts = exchange(member_sums(where, preds, slab, *mix), ("z", "x"))
        part = jnp.sum(parts, axis=0)
        parts = exchange(jnp.broadcast_to(part[None], (16, 16, 128)), ("y", "core"))
        given, plane = solve(repeat == SUBSTEPS - 1, where, parts, slab, *mix)
        mix = [in_vmem(given)]
    return (plane, given)


def solution(mesh):
    grid = Mesh(mesh.devices.reshape(8, 2, 8, 4), ("z", "core", "y", "x"))
    member, point = ("z", "core"), ("y", "x")
    in_specs = (
        P(member, point),
        P(point, None),
        P(),
        P(point),
        P(point),
        P(member, point),
    )
    out_specs = (P(member, point), P())
    return jax.shard_map(local, mesh=grid, in_specs=in_specs, out_specs=out_specs, check_vma=False)
```

```python
import functools

import jax
import jax.numpy as jnp
from jax import lax
from jax.experimental import pallas as pl
from jax.experimental.pallas import tpu as pltpu
from jax.sharding import Mesh, PartitionSpec as P

SENSORS = 1024
WIDTH = 256
BASIS = 512
FEATS = 256
QOBS = 64
SUBSTEPS = 2
MEMBERS = 32
NOISE_STD = 0.5
RIDGE_SHARE = 0.5
ROWS = 40
NOTES = 32
F32, BF16 = jnp.float32, jnp.bfloat16
HIGHEST = lax.Precision.HIGHEST
VMEM = pl.BlockSpec(memory_space=pltpu.VMEM)
SMEM = pl.BlockSpec(memory_space=pltpu.SMEM)


def in_vmem(x):
    return pltpu.with_memory_space_constraint(x, pltpu.VMEM)


def mxu(a, b):
    return jnp.dot(a, b, preferred_element_type=F32)


def prepare_kernel(ensemble_ref, inputs_ref, picks_ref, observed_ref, perturb_ref, own_ref, keep_ref, give_ref, ext_ref):
    core = lax.axis_index("core")
    for i in range(2):
        for e in range(16):
            for part in range(6):
                at = 768 * e + 128 * part
                row, left = 8 * (e // 4) + part, 128 * (e % 4)
                own_ref[i, row : row + 1, left : left + 128] = (
                    observed_ref[0:1, at : at + 128] + perturb_ref[i : i + 1, at : at + 128]
                )
            own_ref[i, 8 * (e // 4) + 6 : 8 * (e // 4) + 8, 128 * (e % 4) : 128 * (e % 4) + 128] = jnp.zeros((2, 128), F32)
        for row in range(ROWS):
            own_ref[i, NOTES + row : NOTES + row + 1, :] = ensemble_ref[i : i + 1, 512 * row : 512 * row + 512]
        keep_ref[i] = own_ref[i, NOTES:, pl.ds(pl.multiple_of(core * 256, 256), 256)].astype(BF16)
        give_ref[i] = own_ref[i, NOTES:, pl.ds(pl.multiple_of((1 - core) * 256, 256), 256)].astype(BF16)
    ext_ref[:, :SENSORS] = inputs_ref[pl.ds(pl.multiple_of(core * 96, 32), 96), :]
    picks = picks_ref[pl.ds(pl.multiple_of(core * 48, 16), 48), :]
    ext_ref[:48, SENSORS:] = picks.astype(F32).astype(BF16)
    ext_ref[48:, SENSORS:] = jnp.zeros((48, 128), BF16)


def prepare(ensemble, inputs, picks, observed, perturb):
    return pl.pallas_call(
        prepare_kernel,
        out_shape=(
            jax.ShapeDtypeStruct((2, NOTES + ROWS, 512), F32),
            pltpu.VMEM((2, ROWS, 256), BF16),
            pltpu.VMEM((2, ROWS, 256), BF16),
            pltpu.VMEM((96, SENSORS + 128), BF16),
        ),
        in_specs=[VMEM] * 5,
        out_specs=(VMEM,) * 4,
        name="prepare",
    )(ensemble, inputs, picks, observed, perturb)


def evaluate_kernel(where_ref, own_ref, other_ref, x_ref, features_ref, out_ref, whole_ref, chosen_ref):
    r = lax.broadcasted_iota(jnp.int32, (256, 256), 0)
    s = lax.broadcasted_iota(jnp.int32, (256, 256), 1)
    mix = (s == ((r + where_ref[1]) % 2) * 128 + r // 2).astype(F32).astype(BF16)

    def narrow(start):
        both = jnp.concatenate([own_ref[start : start + 128, :], other_ref[start : start + 128, :]], 0)
        return mxu(mix, both).astype(BF16)

    branch_in, branch_mid, branch_out, trunk_in, trunk_out = 0, 512, 640, 896, 1024
    halves = (own_ref, other_ref)
    trunk_hidden = jnp.tanh(mxu(features_ref[...], narrow(trunk_in)) * FEATS ** (-0.5)).astype(BF16)
    trunk = [
        (mxu(trunk_hidden, half[trunk_out : trunk_out + 256, :]) * WIDTH ** (-0.5)).astype(BF16) for half in halves
    ]
    total = None
    for i in range(4):
        part = mxu(x_ref[:, 256 * i : 256 * i + 256], narrow(branch_in + 128 * i))
        total = part if total is None else total + part
    hidden = jnp.tanh(total * SENSORS ** (-0.5)).astype(BF16)
    hidden = jnp.tanh(mxu(hidden, narrow(branch_mid)) * WIDTH ** (-0.5)).astype(BF16)
    whole = None
    for c, half in enumerate(halves):
        branch = (mxu(hidden, half[branch_out : branch_out + 256, :]) * WIDTH ** (-0.5)).astype(BF16)
        part = lax.dot_general(branch, trunk[c], (((1,), (1,)), ((), ())), preferred_element_type=F32)
        whole = part if whole is None else whole + part
    whole_ref[...] = whole * BASIS ** (-0.5)
    left = lax.broadcasted_iota(jnp.int32, (48, 128), 1) < QOBS
    for x in range(4):
        picks = x_ref[96 * x : 96 * x + 48, SENSORS:].astype(F32).astype(jnp.int32)
        even = whole_ref[pl.ds(96 * x, 48, stride=2), :]
        odd = whole_ref[pl.ds(96 * x + 1, 48, stride=2), :]
        chosen_ref[48 * x : 48 * x + 48, :] = jnp.where(
            left,
            jnp.take_along_axis(even, picks, axis=1, mode="promise_in_bounds"),
            jnp.take_along_axis(odd, picks, axis=1, mode="promise_in_bounds"),
        )
    for x in range(4):
        for z in range(8):
            at = 48 * x + 6 * z
            out_ref[4 * z + x] = chosen_ref[at : at + 6, :].astype(BF16)


def evaluate(where, own, other, inputs_ext, features):
    return pl.pallas_call(
        evaluate_kernel,
        out_shape=pltpu.VMEM((32, 6, 128), BF16),
        in_specs=[SMEM] + [VMEM] * 4,
        out_specs=VMEM,
        scratch_shapes=[pltpu.VMEM((384, 128), F32), pltpu.VMEM((192, 128), F32)],
        name="evaluate",
    )(where, in_vmem(own), in_vmem(other), in_vmem(inputs_ext), features)


def split(x):
    high = x.astype(BF16)
    rest = x - high.astype(F32)
    middle = rest.astype(BF16)
    return high, middle, (rest - middle.astype(F32)).astype(BF16)


def sums_kernel(where_ref, preds_ref, target_ref, state_ref, *rest):
    *mix_ref, out_ref, preds_f32_ref = rest
    preds_f32_ref[...] = preds_ref[...].astype(F32)
    preds = jnp.concatenate([preds_f32_ref[:, i, :] for i in range(6)], 1)
    target = jnp.concatenate([target_ref[:, i, :] for i in range(6)], 1)
    innov = ((target - preds) / NOISE_STD).astype(BF16)
    anom = (preds - jnp.mean(preds, axis=0, keepdims=True)) / (NOISE_STD * (MEMBERS - 1) ** 0.5)
    state = jnp.concatenate([state_ref[:, i, :] for i in range(8)], 1)
    if mix_ref:
        state = jnp.dot(mix_ref[0][...], state, precision=HIGHEST, preferred_element_type=F32)
    share = where_ref[6].astype(F32)
    par_anom = (state - jnp.mean(state, axis=0, keepdims=True)) * (share / (MEMBERS - 1) ** 0.5)
    lefts = [jnp.concatenate(pair, 1) for pair in zip(split(anom), split(par_anom))]
    nothing = jnp.zeros_like(innov)
    rights = [jnp.concatenate(pair, 1) for pair in zip((innov, nothing, nothing), split(-state))]
    lhs = jnp.concatenate(lefts, 0)
    rhs = jnp.concatenate([term for pair in zip(lefts, rights) for term in pair], 0)
    terms = lax.dot_general(lhs, rhs, (((1,), (1,)), ((), ())), preferred_element_type=F32)
    terms = terms[0:32] + terms[32:64] + terms[64:96]
    both = terms[:, 0:64] + terms[:, 64:128] + terms[:, 128:192]
    packed = jnp.concatenate([both[0:16], both[16:32]], 1)
    for i in range(32):
        out_ref[i] = packed


def member_sums(where, preds, slab, *mix):
    whole = lambda shape: pl.BlockSpec(shape, lambda i, w: (0,) * len(shape))
    return pl.pallas_call(
        sums_kernel,
        out_shape=pltpu.VMEM((32, 16, 128), F32),
        grid_spec=pltpu.PrefetchScalarGridSpec(
            num_scalar_prefetch=1,
            grid=(1,),
            in_specs=[
                whole((32, 6, 128)),
                pl.BlockSpec((32, 8, 128), lambda i, w: (0, w[3], w[4])),
                pl.BlockSpec((32, 8, 256), lambda i, w: (0, w[5], w[7])),
            ]
            + [whole((32, 32)) for _ in mix],
            out_specs=whole((32, 16, 128)),
            scratch_shapes=[pltpu.VMEM((32, 6, 128), F32)],
        ),
        name="member_sums",
    )(where, in_vmem(preds), slab, slab, *mix)


def solve_kernel(last, where_ref, parts_ref, slab_ref, *rest):
    *mix_ref, given_ref, state_ref, held_ref, step_ref, sem = rest
    if last:
        wanted = slab_ref.at[:, pl.ds(NOTES, ROWS), :]
    else:
        wanted = slab_ref.at[:, pl.ds(NOTES, ROWS), pl.ds(pl.multiple_of(where_ref[1] * 256, 256), 256)]
    fetch = pltpu.make_async_copy(wanted, held_ref, sem)
    fetch.start()
    both = parts_ref[0]
    for i in range(1, 16):
        both = both + parts_ref[i]
    gram = jnp.concatenate([both[:, 0:32], both[:, 64:96]], 0)
    cross = jnp.concatenate([both[:, 32:64], both[:, 96:128]], 0)
    r = lax.broadcasted_iota(jnp.int32, (32, 32), 0)
    s = lax.broadcasted_iota(jnp.int32, (32, 32), 1)
    eye = (r == s).astype(F32)
    trace = jnp.sum(jnp.sum(gram * eye, axis=1, keepdims=True), axis=0, keepdims=True)
    system = gram + (RIDGE_SHARE / MEMBERS) * trace * eye
    table = jnp.concatenate([system, cross], 1)
    line = lax.broadcasted_iota(jnp.int32, (32, 64), 0)
    for k in range(0, 32, 2):
        first = jnp.broadcast_to(table[:, k : k + 1], (32, 64))
        second = jnp.broadcast_to(table[:, k + 1 : k + 2], (32, 64))
        upper, lower = table[k : k + 1, :], table[k + 1 : k + 2, :]
        a, b, c, d = first[k : k + 1], second[k : k + 1], first[k + 1 : k + 2], second[k + 1 : k + 2]
        inverse = 1.0 / (a * d - b * c)
        new_upper = (d * upper - b * lower) * inverse
        new_lower = (a * lower - c * upper) * inverse
        rest = table - first * new_upper - second * new_lower
        table = jnp.where(line == k, new_upper, jnp.where(line == k + 1, new_lower, rest))
    coefficients = table[:, 32:64]
    turned = lax.dot_general(
        coefficients, eye, (((0,), (0,)), ((), ())), precision=HIGHEST, preferred_element_type=F32
    )
    centred = turned - jnp.mean(turned, axis=1, keepdims=True)
    step = eye + centred / (MEMBERS - 1) ** 0.5
    if mix_ref:
        step = jnp.dot(step, mix_ref[0][...], precision=HIGHEST, preferred_element_type=F32)
    step_ref[...] = step
    given_ref[...] = coefficients if last else step
    count = 2 if last else 4
    rows = step_ref[pl.ds(where_ref[2 if last else 0], count), :]
    fetch.wait()
    for i in range(count):
        total = None
        for j in range(MEMBERS):
            part = rows[i : i + 1, j : j + 1] * held_ref[j]
            total = part if total is None else total + part
        if last:
            for row in range(ROWS):
                state_ref[i : i + 1, 512 * row : 512 * row + 512] = total[row : row + 1, :]
        else:
            for y in range(8):
                state_ref[y, i] = total.astype(BF16)


def solve(last, where, parts, slab, *mix):
    if last:
        outs = jax.ShapeDtypeStruct((32, 32), F32), jax.ShapeDtypeStruct((2, ROWS * 512), F32)
    else:
        outs = pltpu.VMEM((32, 32), F32), pltpu.VMEM((8, 4, ROWS, 256), BF16)
    return pl.pallas_call(
        functools.partial(solve_kernel, last),
        out_shape=outs,
        in_specs=[SMEM, VMEM, pl.BlockSpec(memory_space=pl.ANY)] + [VMEM for _ in mix],
        out_specs=(VMEM,) * 2,
        scratch_shapes=[
            pltpu.VMEM((MEMBERS, ROWS, 512 if last else 256), F32),
            pltpu.VMEM((32, 32), F32),
            pltpu.SemaphoreType.DMA,
        ],
        name="solve",
    )(where, in_vmem(parts), slab, *mix)


def exchange(blocks, axes):
    return lax.all_to_all(blocks, axes, 0, 0, tiled=True)


def swap(block):
    return lax.ppermute(block, "core", [(0, 1), (1, 0)])


def local(ensemble, inputs, features, query_index, observed, perturb):
    z, core = lax.axis_index("z"), lax.axis_index("core")
    e, block = z * 2 + core, core * 8 + z
    where = jnp.stack(
        [4 * z, core, 2 * e, block // 4, block % 4, 4 + jnp.minimum(e, 9) // 2, (e < 10).astype(jnp.int32), e % 2]
    )
    own, keep, give, ext = prepare(
        ensemble, inputs, query_index.reshape(96, 128), observed.reshape(1, -1), perturb
    )
    slab = lax.all_gather(own, ("z", "core"), axis=0, tiled=True)
    taken = swap(give)
    plane = jnp.where(core == 0, jnp.concatenate([keep, taken]), jnp.concatenate([taken, keep]))
    plane = jnp.broadcast_to(plane[None], (8, 4, ROWS, 256))
    ext = lax.all_gather(ext, "x", axis=0, tiled=True)
    mix = []
    for repeat in range(SUBSTEPS):
        half = exchange(plane.reshape(32, ROWS, 256), ("y", "x")).reshape(32 * ROWS, 256)
        half, ext = lax.optimization_barrier((half, ext))
        other = swap(half)
        preds = evaluate(where, half, other, ext, features)
        preds = exchange(preds, ("z", "x"))
        parts = exchange(member_sums(where, preds, slab, *mix), ("x", "z"))
        part = jnp.sum(parts, axis=0)
        parts = exchange(jnp.broadcast_to(part[None], (16, 16, 128)), ("core", "y"))
        given, plane = solve(repeat == SUBSTEPS - 1, where, parts, slab, *mix)
        mix = [in_vmem(given)]
    return (plane, given)


def solution(mesh):
    grid = Mesh(mesh.devices.reshape(8, 2, 8, 4), ("z", "core", "y", "x"))
    member, point = ("z", "core"), ("y", "x")
    in_specs = (
        P(member, point),
        P(point, None),
        P(),
        P(point),
        P(point),
        P(member, point),
    )
    out_specs = (P(member, point), P())
    return jax.shard_map(local, mesh=grid, in_specs=in_specs, out_specs=out_specs, check_vma=False)
```

```python
import functools

import jax
import jax.numpy as jnp
from jax import lax
from jax.experimental import pallas as pl
from jax.experimental.pallas import tpu as pltpu
from jax.sharding import Mesh, PartitionSpec as P

SENSORS = 1024
WIDTH = 256
BASIS = 512
FEATS = 256
QOBS = 64
SUBSTEPS = 2
MEMBERS = 32
NOISE_STD = 0.5
RIDGE_SHARE = 0.5
ROWS = 40
NOTES = 32
F32, BF16 = jnp.float32, jnp.bfloat16
HIGHEST = lax.Precision.HIGHEST
VMEM = pl.BlockSpec(memory_space=pltpu.VMEM)
ANY = pl.BlockSpec(memory_space=pl.ANY)


def in_vmem(x):
    return pltpu.with_memory_space_constraint(x, pltpu.VMEM)


def mxu(a, b):
    return jnp.dot(a, b, preferred_element_type=F32)


def prepare_kernel(ensemble_ref, inputs_ref, picks_ref, observed_ref, perturb_ref, own_ref, keep_ref, give_ref, ext_ref):
    core = lax.axis_index("core")
    for i in range(2):
        for e in range(16):
            for part in range(6):
                at = 768 * e + 128 * part
                row, left = 8 * (e // 4) + part, 128 * (e % 4)
                own_ref[i, row : row + 1, left : left + 128] = (
                    observed_ref[0:1, at : at + 128] + perturb_ref[i : i + 1, at : at + 128]
                )
            own_ref[i, 8 * (e // 4) + 6 : 8 * (e // 4) + 8, 128 * (e % 4) : 128 * (e % 4) + 128] = jnp.zeros((2, 128), F32)
        for row in range(ROWS):
            own_ref[i, NOTES + row : NOTES + row + 1, :] = ensemble_ref[i : i + 1, 512 * row : 512 * row + 512]
        keep_ref[i] = own_ref[i, NOTES:, pl.ds(pl.multiple_of(core * 256, 256), 256)].astype(BF16)
        give_ref[i] = own_ref[i, NOTES:, pl.ds(pl.multiple_of((1 - core) * 256, 256), 256)].astype(BF16)
    ext_ref[:, :SENSORS] = inputs_ref[pl.ds(pl.multiple_of(core * 96, 32), 96), :]
    picks = picks_ref[pl.ds(pl.multiple_of(core * 48, 16), 48), :]
    ext_ref[:48, SENSORS:] = picks.astype(F32).astype(BF16)
    ext_ref[48:, SENSORS:] = jnp.zeros((48, 128), BF16)


def prepare(ensemble, inputs, picks, observed, perturb):
    return pl.pallas_call(
        prepare_kernel,
        out_shape=(
            jax.ShapeDtypeStruct((2, NOTES + ROWS, 512), F32),
            pltpu.VMEM((2, ROWS, 256), BF16),
            pltpu.VMEM((2, ROWS, 256), BF16),
            pltpu.VMEM((96, SENSORS + 128), BF16),
        ),
        in_specs=[VMEM] * 5,
        out_specs=(VMEM,) * 4,
        name="prepare",
    )(ensemble, inputs, picks, observed, perturb)


def evaluate_kernel(own_ref, other_ref, x_ref, features_hbm, out_ref, whole_ref, chosen_ref, features_ref, sem):
    fetch = pltpu.make_async_copy(features_hbm, features_ref, sem)
    fetch.start()
    r = lax.broadcasted_iota(jnp.int32, (256, 256), 0)
    s = lax.broadcasted_iota(jnp.int32, (256, 256), 1)
    mix = (s == ((r + lax.axis_index("core")) % 2) * 128 + r // 2).astype(F32).astype(BF16)

    def narrow(start):
        both = jnp.concatenate([own_ref[start : start + 128, :], other_ref[start : start + 128, :]], 0)
        return mxu(mix, both).astype(BF16)

    branch_in, branch_mid, branch_out, trunk_in, trunk_out = 0, 512, 640, 896, 1024
    halves = (own_ref, other_ref)
    total = None
    for i in range(4):
        part = mxu(x_ref[:, 256 * i : 256 * i + 256], narrow(branch_in + 128 * i))
        total = part if total is None else total + part
    hidden = jnp.tanh(total * SENSORS ** (-0.5)).astype(BF16)
    hidden = jnp.tanh(mxu(hidden, narrow(branch_mid)) * WIDTH ** (-0.5)).astype(BF16)
    fetch.wait()
    trunk_hidden = jnp.tanh(mxu(features_ref[...], narrow(trunk_in)) * FEATS ** (-0.5)).astype(BF16)
    trunk = [
        (mxu(trunk_hidden, half[trunk_out : trunk_out + 256, :]) * WIDTH ** (-0.5)).astype(BF16) for half in halves
    ]
    whole = None
    for c, half in enumerate(halves):
        branch = (mxu(hidden, half[branch_out : branch_out + 256, :]) * WIDTH ** (-0.5)).astype(BF16)
        part = lax.dot_general(branch, trunk[c], (((1,), (1,)), ((), ())), preferred_element_type=F32)
        whole = part if whole is None else whole + part
    whole_ref[...] = whole * BASIS ** (-0.5)
    left = lax.broadcasted_iota(jnp.int32, (48, 128), 1) < QOBS
    for x in range(4):
        picks = x_ref[96 * x : 96 * x + 48, SENSORS:].astype(F32).astype(jnp.int32)
        even = whole_ref[pl.ds(96 * x, 48, stride=2), :]
        odd = whole_ref[pl.ds(96 * x + 1, 48, stride=2), :]
        chosen_ref[48 * x : 48 * x + 48, :] = jnp.where(
            left,
            jnp.take_along_axis(even, picks, axis=1, mode="promise_in_bounds"),
            jnp.take_along_axis(odd, picks, axis=1, mode="promise_in_bounds"),
        )
    for x in range(4):
        for z in range(8):
            at = 48 * x + 6 * z
            out_ref[4 * z + x] = chosen_ref[at : at + 6, :].astype(BF16)


def evaluate(own, other, inputs_ext, features):
    return pl.pallas_call(
        evaluate_kernel,
        out_shape=pltpu.VMEM((32, 6, 128), BF16),
        in_specs=[VMEM] * 3 + [ANY],
        out_specs=VMEM,
        scratch_shapes=[
            pltpu.VMEM((384, 128), F32),
            pltpu.VMEM((192, 128), F32),
            pltpu.VMEM((128, FEATS), BF16),
            pltpu.SemaphoreType.DMA,
        ],
        name="evaluate",
    )(in_vmem(own), in_vmem(other), in_vmem(inputs_ext), features)


def split(x):
    high = x.astype(BF16)
    rest = x - high.astype(F32)
    middle = rest.astype(BF16)
    return high, middle, (rest - middle.astype(F32)).astype(BF16)


def sums_kernel(preds_ref, slab_ref, *rest):
    *mix_hbm, out_ref, preds_f32_ref, target_ref, state_ref, mix_ref, sems = rest
    z, core = lax.axis_index("z"), lax.axis_index("core")
    block = core * 8 + z
    place = z * 2 + core
    share = (place < 10).astype(F32)
    place = jnp.minimum(place, 9)
    row = pl.multiple_of(8 * (block // 4), 8)
    column = pl.multiple_of(128 * (block % 4), 128)
    fetches = [
        pltpu.make_async_copy(slab_ref.at[:, pl.ds(row, 8), pl.ds(column, 128)], target_ref, sems.at[0])
    ]
    row = pl.multiple_of(NOTES + 8 * (place // 2), 8)
    column = pl.multiple_of(256 * (place % 2), 256)
    fetches.append(
        pltpu.make_async_copy(slab_ref.at[:, pl.ds(row, 8), pl.ds(column, 256)], state_ref, sems.at[1])
    )
    if mix_hbm:
        fetches.append(pltpu.make_async_copy(mix_hbm[0], mix_ref, sems.at[2]))
    for fetch in fetches:
        fetch.start()
    preds_f32_ref[...] = preds_ref[...].astype(F32)
    preds = jnp.concatenate([preds_f32_ref[:, i, :] for i in range(6)], 1)
    anom = (preds - jnp.mean(preds, axis=0, keepdims=True)) / (NOISE_STD * (MEMBERS - 1) ** 0.5)
    lefts_seen = split(anom)
    for fetch in fetches:
        fetch.wait()
    target = jnp.concatenate([target_ref[:, i, :] for i in range(6)], 1)
    innov = ((target - preds) / NOISE_STD).astype(BF16)
    state = jnp.concatenate([state_ref[:, i, :] for i in range(8)], 1)
    if mix_hbm:
        state = jnp.dot(mix_ref[...], state, precision=HIGHEST, preferred_element_type=F32)
    par_anom = (state - jnp.mean(state, axis=0, keepdims=True)) * (share / (MEMBERS - 1) ** 0.5)
    lefts = [jnp.concatenate(pair, 1) for pair in zip(lefts_seen, split(par_anom))]
    nothing = jnp.zeros_like(innov)
    rights = [jnp.concatenate(pair, 1) for pair in zip((innov, nothing, nothing), split(-state))]
    lhs = jnp.concatenate(lefts, 0)
    rhs = jnp.concatenate([term for pair in zip(lefts, rights) for term in pair], 0)
    terms = lax.dot_general(lhs, rhs, (((1,), (1,)), ((), ())), preferred_element_type=F32)
    terms = terms[0:32] + terms[32:64] + terms[64:96]
    both = terms[:, 0:64] + terms[:, 64:128] + terms[:, 128:192]
    packed = jnp.concatenate([both[0:16], both[16:32]], 1)
    for i in range(32):
        out_ref[i] = packed


def member_sums(preds, slab, *mix):
    return pl.pallas_call(
        sums_kernel,
        out_shape=pltpu.VMEM((32, 16, 128), F32),
        in_specs=[VMEM, ANY] + [ANY for _ in mix],
        out_specs=VMEM,
        scratch_shapes=[
            pltpu.VMEM((32, 6, 128), F32),
            pltpu.VMEM((32, 8, 128), F32),
            pltpu.VMEM((32, 8, 256), F32),
            pltpu.VMEM((32, 32), F32),
            pltpu.SemaphoreType.DMA((3,)),
        ],
        name="member_sums",
    )(in_vmem(preds), slab, *mix)


def solve_kernel(last, parts_ref, slab_ref, *rest):
    *mix_hbm, given_ref, state_ref, held_ref, step_ref, mix_ref, sem, mix_sem = rest
    z, core = lax.axis_index("z"), lax.axis_index("core")
    if mix_hbm:
        mix_fetch = pltpu.make_async_copy(mix_hbm[0], mix_ref, mix_sem)
        mix_fetch.start()
    if last:
        wanted = slab_ref.at[:, pl.ds(NOTES, ROWS), :]
    else:
        wanted = slab_ref.at[:, pl.ds(NOTES, ROWS), pl.ds(pl.multiple_of(core * 256, 256), 256)]
    fetch = pltpu.make_async_copy(wanted, held_ref, sem)
    fetch.start()
    both = parts_ref[0]
    for i in range(1, 16):
        both = both + parts_ref[i]
    gram = jnp.concatenate([both[:, 0:32], both[:, 64:96]], 0)
    cross = jnp.concatenate([both[:, 32:64], both[:, 96:128]], 0)
    r = lax.broadcasted_iota(jnp.int32, (32, 32), 0)
    s = lax.broadcasted_iota(jnp.int32, (32, 32), 1)
    eye = (r == s).astype(F32)
    trace = jnp.sum(jnp.sum(gram * eye, axis=1, keepdims=True), axis=0, keepdims=True)
    system = gram + (RIDGE_SHARE / MEMBERS) * trace * eye
    table = jnp.concatenate([system, cross], 1)
    line = lax.broadcasted_iota(jnp.int32, (32, 64), 0)
    for k in range(0, 32, 2):
        first = jnp.broadcast_to(table[:, k : k + 1], (32, 64))
        second = jnp.broadcast_to(table[:, k + 1 : k + 2], (32, 64))
        upper, lower = table[k : k + 1, :], table[k + 1 : k + 2, :]
        a, b, c, d = first[k : k + 1], second[k : k + 1], first[k + 1 : k + 2], second[k + 1 : k + 2]
        inverse = 1.0 / (a * d - b * c)
        new_upper = (d * upper - b * lower) * inverse
        new_lower = (a * lower - c * upper) * inverse
        rest = table - first * new_upper - second * new_lower
        table = jnp.where(line == k, new_upper, jnp.where(line == k + 1, new_lower, rest))
    coefficients = table[:, 32:64]
    turned = lax.dot_general(
        coefficients, eye, (((0,), (0,)), ((), ())), precision=HIGHEST, preferred_element_type=F32
    )
    centred = turned - jnp.mean(turned, axis=1, keepdims=True)
    step = eye + centred / (MEMBERS - 1) ** 0.5
    if mix_hbm:
        mix_fetch.wait()
        step = jnp.dot(step, mix_ref[...], precision=HIGHEST, preferred_element_type=F32)
    step_ref[...] = step
    given_ref[...] = coefficients if last else step
    count = 2 if last else 4
    rows = step_ref[pl.ds(z * 4 + core * 2 if last else z * 4, count), :]
    fetch.wait()
    for i in range(count):
        total = None
        for j in range(MEMBERS):
            part = rows[i : i + 1, j : j + 1] * held_ref[j]
            total = part if total is None else total + part
        if last:
            for row in range(ROWS):
                state_ref[i : i + 1, 512 * row : 512 * row + 512] = total[row : row + 1, :]
        else:
            for y in range(8):
                state_ref[y, i] = total.astype(BF16)


def solve(last, parts, slab, *mix):
    if last:
        outs = jax.ShapeDtypeStruct((32, 32), F32), jax.ShapeDtypeStruct((2, ROWS * 512), F32)
    else:
        outs = jax.ShapeDtypeStruct((32, 32), F32), pltpu.VMEM((8, 4, ROWS, 256), BF16)
    return pl.pallas_call(
        functools.partial(solve_kernel, last),
        out_shape=outs,
        in_specs=[VMEM, ANY] + [ANY for _ in mix],
        out_specs=(VMEM,) * 2,
        scratch_shapes=[
            pltpu.VMEM((MEMBERS, ROWS, 512 if last else 256), F32),
            pltpu.VMEM((32, 32), F32),
            pltpu.VMEM((32, 32), F32),
            pltpu.SemaphoreType.DMA,
            pltpu.SemaphoreType.DMA,
        ],
        name="solve",
    )(in_vmem(parts), slab, *mix)


def exchange(blocks, axes):
    return lax.all_to_all(blocks, axes, 0, 0, tiled=True)


def swap(block):
    return lax.ppermute(block, "core", [(0, 1), (1, 0)])


def local(ensemble, inputs, features, query_index, observed, perturb):
    core = lax.axis_index("core")
    own, keep, give, ext = prepare(
        ensemble, inputs, query_index.reshape(96, 128), observed.reshape(1, -1), perturb
    )
    slab = lax.all_gather(own, ("z", "core"), axis=0, tiled=True)
    taken = swap(give)
    plane = jnp.where(core == 0, jnp.concatenate([keep, taken]), jnp.concatenate([taken, keep]))
    plane = jnp.broadcast_to(plane[None], (8, 4, ROWS, 256))
    ext = lax.all_gather(ext, "x", axis=0, tiled=True)
    mix = []
    for repeat in range(SUBSTEPS):
        half = exchange(plane.reshape(32, ROWS, 256), ("y", "x")).reshape(32 * ROWS, 256)
        half, ext = lax.optimization_barrier((half, ext))
        other = swap(half)
        preds = evaluate(half, other, ext, features)
        preds = exchange(preds, ("z", "x"))
        parts = exchange(member_sums(preds, slab, *mix), ("x", "z"))
        part = jnp.sum(parts, axis=0)
        parts = exchange(jnp.broadcast_to(part[None], (16, 16, 128)), ("core", "y"))
        given, plane = solve(repeat == SUBSTEPS - 1, parts, slab, *mix)
        mix = [given]
    return (plane, given)


def solution(mesh):
    grid = Mesh(mesh.devices.reshape(8, 2, 8, 4), ("z", "core", "y", "x"))
    member, point = ("z", "core"), ("y", "x")
    in_specs = (
        P(member, point),
        P(point, None),
        P(),
        P(point),
        P(point),
        P(member, point),
    )
    out_specs = (P(member, point), P())
    return jax.shard_map(local, mesh=grid, in_specs=in_specs, out_specs=out_specs, check_vma=False)
```

```python
import functools

import jax
import jax.numpy as jnp
from jax import lax
from jax.experimental import pallas as pl
from jax.experimental.pallas import tpu as pltpu
from jax.sharding import Mesh, PartitionSpec as P

SENSORS = 1024
WIDTH = 256
BASIS = 512
FEATS = 256
QOBS = 64
SUBSTEPS = 2
MEMBERS = 32
NOISE_STD = 0.5
RIDGE_SHARE = 0.5
ROWS = 40
NOTES = 32
F32, BF16 = jnp.float32, jnp.bfloat16
HIGHEST = lax.Precision.HIGHEST
VMEM = pl.BlockSpec(memory_space=pltpu.VMEM)
ANY = pl.BlockSpec(memory_space=pl.ANY)


def in_vmem(x):
    return pltpu.with_memory_space_constraint(x, pltpu.VMEM)


def mxu(a, b):
    return jnp.dot(a, b, preferred_element_type=F32)


def prepare_kernel(ensemble_ref, inputs_ref, picks_ref, observed_ref, perturb_ref, own_ref, keep_ref, give_ref, ext_ref):
    core = lax.axis_index("core")
    for i in range(2):
        for e in range(16):
            for part in range(6):
                at = 768 * e + 128 * part
                row, left = 8 * (e // 4) + part, 128 * (e % 4)
                own_ref[i, row : row + 1, left : left + 128] = (
                    observed_ref[0:1, at : at + 128] + perturb_ref[i : i + 1, at : at + 128]
                )
            own_ref[i, 8 * (e // 4) + 6 : 8 * (e // 4) + 8, 128 * (e % 4) : 128 * (e % 4) + 128] = jnp.zeros((2, 128), F32)
        for row in range(ROWS):
            own_ref[i, NOTES + row : NOTES + row + 1, :] = ensemble_ref[i : i + 1, 512 * row : 512 * row + 512]
        keep_ref[i] = own_ref[i, NOTES:, pl.ds(pl.multiple_of(core * 256, 256), 256)].astype(BF16)
        give_ref[i] = own_ref[i, NOTES:, pl.ds(pl.multiple_of((1 - core) * 256, 256), 256)].astype(BF16)
    ext_ref[:, :SENSORS] = inputs_ref[pl.ds(pl.multiple_of(core * 96, 32), 96), :]
    picks = picks_ref[pl.ds(pl.multiple_of(core * 48, 16), 48), :]
    ext_ref[:48, SENSORS:] = picks.astype(F32).astype(BF16)
    ext_ref[48:, SENSORS:] = jnp.zeros((48, 128), BF16)


def prepare(ensemble, inputs, picks, observed, perturb):
    return pl.pallas_call(
        prepare_kernel,
        out_shape=(
            jax.ShapeDtypeStruct((2, NOTES + ROWS, 512), F32),
            pltpu.VMEM((2, ROWS, 256), BF16),
            pltpu.VMEM((2, ROWS, 256), BF16),
            pltpu.VMEM((96, SENSORS + 128), BF16),
        ),
        in_specs=[VMEM] * 5,
        out_specs=(VMEM,) * 4,
        name="prepare",
    )(ensemble, inputs, picks, observed, perturb)


def evaluate_kernel(own_ref, other_ref, x_ref, features_hbm, out_ref, whole_ref, chosen_ref, features_ref, sem):
    fetch = pltpu.make_async_copy(features_hbm, features_ref, sem)
    fetch.start()
    r = lax.broadcasted_iota(jnp.int32, (256, 256), 0)
    s = lax.broadcasted_iota(jnp.int32, (256, 256), 1)
    mix = (s == ((r + lax.axis_index("core")) % 2) * 128 + r // 2).astype(F32).astype(BF16)

    def narrow(start):
        both = jnp.concatenate([own_ref[start : start + 128, :], other_ref[start : start + 128, :]], 0)
        return mxu(mix, both).astype(BF16)

    branch_in, branch_mid, branch_out, trunk_in, trunk_out = 0, 512, 640, 896, 1024
    halves = (own_ref, other_ref)
    total = None
    for i in range(4):
        part = mxu(x_ref[:, 256 * i : 256 * i + 256], narrow(branch_in + 128 * i))
        total = part if total is None else total + part
    hidden = jnp.tanh(total * SENSORS ** (-0.5)).astype(BF16)
    hidden = jnp.tanh(mxu(hidden, narrow(branch_mid)) * WIDTH ** (-0.5)).astype(BF16)
    fetch.wait()
    trunk_hidden = jnp.tanh(mxu(features_ref[...], narrow(trunk_in)) * FEATS ** (-0.5)).astype(BF16)
    trunk = [
        (mxu(trunk_hidden, half[trunk_out : trunk_out + 256, :]) * WIDTH ** (-0.5)).astype(BF16) for half in halves
    ]
    whole = None
    for c, half in enumerate(halves):
        branch = (mxu(hidden, half[branch_out : branch_out + 256, :]) * WIDTH ** (-0.5)).astype(BF16)
        part = lax.dot_general(branch, trunk[c], (((1,), (1,)), ((), ())), preferred_element_type=F32)
        whole = part if whole is None else whole + part
    whole_ref[...] = whole * BASIS ** (-0.5)
    left = lax.broadcasted_iota(jnp.int32, (48, 128), 1) < QOBS
    for x in range(4):
        picks = x_ref[96 * x : 96 * x + 48, SENSORS:].astype(F32).astype(jnp.int32)
        even = whole_ref[pl.ds(96 * x, 48, stride=2), :]
        odd = whole_ref[pl.ds(96 * x + 1, 48, stride=2), :]
        chosen_ref[48 * x : 48 * x + 48, :] = jnp.where(
            left,
            jnp.take_along_axis(even, picks, axis=1, mode="promise_in_bounds"),
            jnp.take_along_axis(odd, picks, axis=1, mode="promise_in_bounds"),
        )
    for x in range(4):
        for z in range(8):
            at = 48 * x + 6 * z
            out_ref[4 * z + x] = chosen_ref[at : at + 6, :].astype(BF16)


def evaluate(own, other, inputs_ext, features):
    return pl.pallas_call(
        evaluate_kernel,
        out_shape=pltpu.VMEM((32, 6, 128), BF16),
        in_specs=[VMEM] * 3 + [ANY],
        out_specs=VMEM,
        scratch_shapes=[
            pltpu.VMEM((384, 128), F32),
            pltpu.VMEM((192, 128), F32),
            pltpu.VMEM((128, FEATS), BF16),
            pltpu.SemaphoreType.DMA,
        ],
        name="evaluate",
    )(in_vmem(own), in_vmem(other), in_vmem(inputs_ext), features)


def split(x):
    high = x.astype(BF16)
    rest = x - high.astype(F32)
    middle = rest.astype(BF16)
    return high, middle, (rest - middle.astype(F32)).astype(BF16)


def sums_kernel(preds_ref, slab_ref, *rest):
    *mix_hbm, out_ref, preds_f32_ref, target_ref, state_ref, mix_ref, sems = rest
    z, core = lax.axis_index("z"), lax.axis_index("core")
    block = core * 8 + z
    place = z * 2 + core
    share = (place < 10).astype(F32)
    place = jnp.minimum(place, 9)
    row = pl.multiple_of(8 * (block // 4), 8)
    column = pl.multiple_of(128 * (block % 4), 128)
    fetches = [
        pltpu.make_async_copy(slab_ref.at[:, pl.ds(row, 8), pl.ds(column, 128)], target_ref, sems.at[0])
    ]
    row = pl.multiple_of(NOTES + 8 * (place // 2), 8)
    column = pl.multiple_of(256 * (place % 2), 256)
    fetches.append(
        pltpu.make_async_copy(slab_ref.at[:, pl.ds(row, 8), pl.ds(column, 256)], state_ref, sems.at[1])
    )
    if mix_hbm:
        fetches.append(pltpu.make_async_copy(mix_hbm[0], mix_ref, sems.at[2]))
    for fetch in fetches:
        fetch.start()
    preds_f32_ref[...] = preds_ref[...].astype(F32)
    preds = jnp.concatenate([preds_f32_ref[:, i, :] for i in range(6)], 1)
    anom = (preds - jnp.mean(preds, axis=0, keepdims=True)) / (NOISE_STD * (MEMBERS - 1) ** 0.5)
    lefts_seen = split(anom)
    for fetch in fetches:
        fetch.wait()
    target = jnp.concatenate([target_ref[:, i, :] for i in range(6)], 1)
    innov = ((target - preds) / NOISE_STD).astype(BF16)
    state = jnp.concatenate([state_ref[:, i, :] for i in range(8)], 1)
    if mix_hbm:
        state = jnp.dot(mix_ref[...], state, precision=HIGHEST, preferred_element_type=F32)
    par_anom = (state - jnp.mean(state, axis=0, keepdims=True)) * (share / (MEMBERS - 1) ** 0.5)
    lefts = [jnp.concatenate(pair, 1) for pair in zip(lefts_seen, split(par_anom))]
    nothing = jnp.zeros_like(innov)
    rights = [jnp.concatenate(pair, 1) for pair in zip((innov, nothing, nothing), split(-state))]
    lhs = jnp.concatenate(lefts, 0)
    rhs = jnp.concatenate([term for pair in zip(lefts, rights) for term in pair], 0)
    terms = lax.dot_general(lhs, rhs, (((1,), (1,)), ((), ())), preferred_element_type=F32)
    terms = terms[0:32] + terms[32:64] + terms[64:96]
    both = terms[:, 0:64] + terms[:, 64:128] + terms[:, 128:192]
    packed = jnp.concatenate([both[0:16], both[16:32]], 1)
    for i in range(32):
        out_ref[i] = packed


def member_sums(preds, slab, *mix):
    return pl.pallas_call(
        sums_kernel,
        out_shape=pltpu.VMEM((32, 16, 128), F32),
        in_specs=[VMEM, ANY] + [ANY for _ in mix],
        out_specs=VMEM,
        scratch_shapes=[
            pltpu.VMEM((32, 6, 128), F32),
            pltpu.VMEM((32, 8, 128), F32),
            pltpu.VMEM((32, 8, 256), F32),
            pltpu.VMEM((32, 32), F32),
            pltpu.SemaphoreType.DMA((3,)),
        ],
        name="member_sums",
    )(in_vmem(preds), slab, *mix)


STEP = 4


def solve_block(block, right):
    half = len(block) // 2
    if half == 1:
        (a, b), (c, d) = block
        inverse = 1.0 / (a * d - b * c)
        return [
            [(d * u - b * l) * inverse for u, l in zip(*right)],
            [(a * l - c * u) * inverse for u, l in zip(*right)],
        ]

    def less(rows, factors, others):
        return [
            [x - sum(f * o[j] for f, o in zip(factor, others)) for j, x in enumerate(row)]
            for row, factor in zip(rows, factors)
        ]

    upper, lower = block[:half], block[half:]
    solved = solve_block([row[:half] for row in upper], [row[half:] + r for row, r in zip(upper, right)])
    edge, top = [row[:half] for row in solved], [row[half:] for row in solved]
    left = [row[:half] for row in lower]
    bottom = solve_block(less([row[half:] for row in lower], left, edge), less(right[half:], left, top))
    return less(top, edge, bottom) + bottom


def solve_kernel(last, parts_ref, slab_ref, *rest):
    *mix_hbm, given_ref, state_ref, held_ref, step_ref, mix_ref, sem, mix_sem = rest
    z, core = lax.axis_index("z"), lax.axis_index("core")
    if mix_hbm:
        mix_fetch = pltpu.make_async_copy(mix_hbm[0], mix_ref, mix_sem)
        mix_fetch.start()
    if last:
        wanted = slab_ref.at[:, pl.ds(NOTES, ROWS), :]
    else:
        wanted = slab_ref.at[:, pl.ds(NOTES, ROWS), pl.ds(pl.multiple_of(core * 256, 256), 256)]
    fetch = pltpu.make_async_copy(wanted, held_ref, sem)
    fetch.start()
    both = parts_ref[0]
    for i in range(1, 16):
        both = both + parts_ref[i]
    gram = jnp.concatenate([both[:, 0:32], both[:, 64:96]], 0)
    cross = jnp.concatenate([both[:, 32:64], both[:, 96:128]], 0)
    r = lax.broadcasted_iota(jnp.int32, (32, 32), 0)
    s = lax.broadcasted_iota(jnp.int32, (32, 32), 1)
    eye = (r == s).astype(F32)
    trace = jnp.sum(jnp.sum(gram * eye, axis=1, keepdims=True), axis=0, keepdims=True)
    system = gram + (RIDGE_SHARE / MEMBERS) * trace * eye
    table = jnp.concatenate([system, cross], 1)
    line = lax.broadcasted_iota(jnp.int32, (32, 64), 0)
    for k in range(0, 32, STEP):
        columns = [jnp.broadcast_to(table[:, k + j : k + j + 1], (32, 64)) for j in range(STEP)]
        block = [[column[k + i : k + i + 1] for column in columns] for i in range(STEP)]
        rows = solve_block(block, [[table[k + i : k + i + 1, :]] for i in range(STEP)])
        for column, (row,) in zip(columns, rows):
            table = table - column * row
        for i, (row,) in enumerate(rows):
            table = jnp.where(line == k + i, row, table)
    coefficients = table[:, 32:64]
    turned = lax.dot_general(
        coefficients, eye, (((0,), (0,)), ((), ())), precision=HIGHEST, preferred_element_type=F32
    )
    centred = turned - jnp.mean(turned, axis=1, keepdims=True)
    step = eye + centred / (MEMBERS - 1) ** 0.5
    if mix_hbm:
        mix_fetch.wait()
        step = jnp.dot(step, mix_ref[...], precision=HIGHEST, preferred_element_type=F32)
    step_ref[...] = step
    given_ref[...] = coefficients if last else step
    count = 2 if last else 4
    rows = step_ref[pl.ds(z * 4 + core * 2 if last else z * 4, count), :]
    fetch.wait()
    for i in range(count):
        total = None
        for j in range(MEMBERS):
            part = rows[i : i + 1, j : j + 1] * held_ref[j]
            total = part if total is None else total + part
        if last:
            for row in range(ROWS):
                state_ref[i : i + 1, 512 * row : 512 * row + 512] = total[row : row + 1, :]
        else:
            for y in range(8):
                state_ref[y, i] = total.astype(BF16)


def solve(last, parts, slab, *mix):
    if last:
        outs = jax.ShapeDtypeStruct((32, 32), F32), jax.ShapeDtypeStruct((2, ROWS * 512), F32)
    else:
        outs = jax.ShapeDtypeStruct((32, 32), F32), pltpu.VMEM((8, 4, ROWS, 256), BF16)
    return pl.pallas_call(
        functools.partial(solve_kernel, last),
        out_shape=outs,
        in_specs=[VMEM, ANY] + [ANY for _ in mix],
        out_specs=(VMEM,) * 2,
        scratch_shapes=[
            pltpu.VMEM((MEMBERS, ROWS, 512 if last else 256), F32),
            pltpu.VMEM((32, 32), F32),
            pltpu.VMEM((32, 32), F32),
            pltpu.SemaphoreType.DMA,
            pltpu.SemaphoreType.DMA,
        ],
        name="solve",
    )(in_vmem(parts), slab, *mix)


def exchange(blocks, axes):
    return lax.all_to_all(blocks, axes, 0, 0, tiled=True)


def swap(block):
    return lax.ppermute(block, "core", [(0, 1), (1, 0)])


def local(ensemble, inputs, features, query_index, observed, perturb):
    core = lax.axis_index("core")
    own, keep, give, ext = prepare(
        ensemble, inputs, query_index.reshape(96, 128), observed.reshape(1, -1), perturb
    )
    slab = lax.all_gather(own, ("z", "core"), axis=0, tiled=True)
    taken = swap(give)
    plane = jnp.where(core == 0, jnp.concatenate([keep, taken]), jnp.concatenate([taken, keep]))
    plane = jnp.broadcast_to(plane[None], (8, 4, ROWS, 256))
    ext = lax.all_gather(ext, "x", axis=0, tiled=True)
    mix = []
    for repeat in range(SUBSTEPS):
        half = exchange(plane.reshape(32, ROWS, 256), ("y", "x")).reshape(32 * ROWS, 256)
        half, ext = lax.optimization_barrier((half, ext))
        other = swap(half)
        preds = evaluate(half, other, ext, features)
        preds = exchange(preds, ("z", "x"))
        parts = exchange(member_sums(preds, slab, *mix), ("x", "z"))
        part = jnp.sum(parts, axis=0)
        parts = exchange(jnp.broadcast_to(part[None], (16, 16, 128)), ("core", "y"))
        given, plane = solve(repeat == SUBSTEPS - 1, parts, slab, *mix)
        mix = [given]
    return (plane, given)


def solution(mesh):
    grid = Mesh(mesh.devices.reshape(8, 2, 8, 4), ("z", "core", "y", "x"))
    member, point = ("z", "core"), ("y", "x")
    in_specs = (
        P(member, point),
        P(point, None),
        P(),
        P(point),
        P(point),
        P(member, point),
    )
    out_specs = (P(member, point), P())
    return jax.shard_map(local, mesh=grid, in_specs=in_specs, out_specs=out_specs, check_vma=False)
```

```python
import functools

import jax
import jax.numpy as jnp
from jax import lax
from jax.experimental import pallas as pl
from jax.experimental.pallas import tpu as pltpu
from jax.sharding import Mesh, PartitionSpec as P

SENSORS = 1024
WIDTH = 256
BASIS = 512
FEATS = 256
QOBS = 64
SUBSTEPS = 2
MEMBERS = 32
NOISE_STD = 0.5
RIDGE_SHARE = 0.5
ROWS = 40
NOTES = 32
F32, BF16 = jnp.float32, jnp.bfloat16
HIGHEST = lax.Precision.HIGHEST
VMEM = pl.BlockSpec(memory_space=pltpu.VMEM)
ANY = pl.BlockSpec(memory_space=pl.ANY)


def in_vmem(x):
    return pltpu.with_memory_space_constraint(x, pltpu.VMEM)


def mxu(a, b):
    return jnp.dot(a, b, preferred_element_type=F32)


def prepare_kernel(ensemble_ref, inputs_ref, picks_ref, observed_ref, perturb_ref, own_ref, keep_ref, give_ref, ext_ref):
    core = lax.axis_index("core")
    for i in range(2):
        for e in range(16):
            for part in range(6):
                at = 768 * e + 128 * part
                row, left = 8 * (e // 4) + part, 128 * (e % 4)
                own_ref[i, row : row + 1, left : left + 128] = (
                    observed_ref[0:1, at : at + 128] + perturb_ref[i : i + 1, at : at + 128]
                )
            own_ref[i, 8 * (e // 4) + 6 : 8 * (e // 4) + 8, 128 * (e % 4) : 128 * (e % 4) + 128] = jnp.zeros((2, 128), F32)
        for row in range(ROWS):
            own_ref[i, NOTES + row : NOTES + row + 1, :] = ensemble_ref[i : i + 1, 512 * row : 512 * row + 512]
        keep_ref[i] = own_ref[i, NOTES:, pl.ds(pl.multiple_of(core * 256, 256), 256)].astype(BF16)
        give_ref[i] = own_ref[i, NOTES:, pl.ds(pl.multiple_of((1 - core) * 256, 256), 256)].astype(BF16)
    ext_ref[:, :SENSORS] = inputs_ref[pl.ds(pl.multiple_of(core * 96, 32), 96), :]
    picks = picks_ref[pl.ds(pl.multiple_of(core * 48, 16), 48), :]
    ext_ref[:48, SENSORS:] = picks.astype(F32).astype(BF16)
    ext_ref[48:, SENSORS:] = jnp.zeros((48, 128), BF16)


def prepare(ensemble, inputs, picks, observed, perturb):
    return pl.pallas_call(
        prepare_kernel,
        out_shape=(
            jax.ShapeDtypeStruct((2, NOTES + ROWS, 512), F32),
            pltpu.VMEM((2, ROWS, 256), BF16),
            pltpu.VMEM((2, ROWS, 256), BF16),
            pltpu.VMEM((96, SENSORS + 128), BF16),
        ),
        in_specs=[VMEM] * 5,
        out_specs=(VMEM,) * 4,
        name="prepare",
    )(ensemble, inputs, picks, observed, perturb)


def evaluate_kernel(own_ref, other_ref, x_ref, features_hbm, out_ref, whole_ref, chosen_ref, features_ref, sem):
    fetch = pltpu.make_async_copy(features_hbm, features_ref, sem)
    fetch.start()
    r = lax.broadcasted_iota(jnp.int32, (256, 256), 0)
    s = lax.broadcasted_iota(jnp.int32, (256, 256), 1)
    mix = (s == ((r + lax.axis_index("core")) % 2) * 128 + r // 2).astype(F32).astype(BF16)

    def narrow(start):
        both = jnp.concatenate([own_ref[start : start + 128, :], other_ref[start : start + 128, :]], 0)
        return mxu(mix, both).astype(BF16)

    branch_in, branch_mid, branch_out, trunk_in, trunk_out = 0, 512, 640, 896, 1024
    halves = (own_ref, other_ref)
    total = None
    for i in range(4):
        part = mxu(x_ref[:, 256 * i : 256 * i + 256], narrow(branch_in + 128 * i))
        total = part if total is None else total + part
    hidden = jnp.tanh(total * SENSORS ** (-0.5)).astype(BF16)
    hidden = jnp.tanh(mxu(hidden, narrow(branch_mid)) * WIDTH ** (-0.5)).astype(BF16)
    fetch.wait()
    trunk_hidden = jnp.tanh(mxu(features_ref[...], narrow(trunk_in)) * FEATS ** (-0.5)).astype(BF16)
    trunk = [
        (mxu(trunk_hidden, half[trunk_out : trunk_out + 256, :]) * WIDTH ** (-0.5)).astype(BF16) for half in halves
    ]
    whole = None
    for c, half in enumerate(halves):
        branch = (mxu(hidden, half[branch_out : branch_out + 256, :]) * WIDTH ** (-0.5)).astype(BF16)
        part = lax.dot_general(branch, trunk[c], (((1,), (1,)), ((), ())), preferred_element_type=F32)
        whole = part if whole is None else whole + part
    whole_ref[...] = whole * BASIS ** (-0.5)
    left = lax.broadcasted_iota(jnp.int32, (48, 128), 1) < QOBS
    for x in range(4):
        picks = x_ref[96 * x : 96 * x + 48, SENSORS:].astype(F32).astype(jnp.int32)
        even = whole_ref[pl.ds(96 * x, 48, stride=2), :]
        odd = whole_ref[pl.ds(96 * x + 1, 48, stride=2), :]
        chosen_ref[48 * x : 48 * x + 48, :] = jnp.where(
            left,
            jnp.take_along_axis(even, picks, axis=1, mode="promise_in_bounds"),
            jnp.take_along_axis(odd, picks, axis=1, mode="promise_in_bounds"),
        )
    for x in range(4):
        for z in range(8):
            at = 48 * x + 6 * z
            out_ref[4 * z + x] = chosen_ref[at : at + 6, :].astype(BF16)


def evaluate(own, other, inputs_ext, features):
    return pl.pallas_call(
        evaluate_kernel,
        out_shape=pltpu.VMEM((32, 6, 128), BF16),
        in_specs=[VMEM] * 3 + [ANY],
        out_specs=VMEM,
        scratch_shapes=[
            pltpu.VMEM((384, 128), F32),
            pltpu.VMEM((192, 128), F32),
            pltpu.VMEM((128, FEATS), BF16),
            pltpu.SemaphoreType.DMA,
        ],
        name="evaluate",
    )(in_vmem(own), in_vmem(other), in_vmem(inputs_ext), features)


def split(x):
    high = x.astype(BF16)
    rest = x - high.astype(F32)
    middle = rest.astype(BF16)
    return high, middle, (rest - middle.astype(F32)).astype(BF16)


def sums_kernel(preds_ref, slab_ref, *rest):
    *mix_hbm, out_ref, preds_f32_ref, target_ref, state_ref, mix_ref, sems = rest
    z, core = lax.axis_index("z"), lax.axis_index("core")
    block = core * 8 + z
    place = z * 2 + core
    share = (place < 10).astype(F32)
    place = jnp.minimum(place, 9)
    row = pl.multiple_of(8 * (block // 4), 8)
    column = pl.multiple_of(128 * (block % 4), 128)
    fetches = [
        pltpu.make_async_copy(slab_ref.at[:, pl.ds(row, 8), pl.ds(column, 128)], target_ref, sems.at[0])
    ]
    row = pl.multiple_of(NOTES + 8 * (place // 2), 8)
    column = pl.multiple_of(256 * (place % 2), 256)
    fetches.append(
        pltpu.make_async_copy(slab_ref.at[:, pl.ds(row, 8), pl.ds(column, 256)], state_ref, sems.at[1])
    )
    if mix_hbm:
        fetches.append(pltpu.make_async_copy(mix_hbm[0], mix_ref, sems.at[2]))
    for fetch in fetches:
        fetch.start()
    preds_f32_ref[...] = preds_ref[...].astype(F32)
    preds = jnp.concatenate([preds_f32_ref[:, i, :] for i in range(6)], 1)
    anom = (preds - jnp.mean(preds, axis=0, keepdims=True)) / (NOISE_STD * (MEMBERS - 1) ** 0.5)
    lefts_seen = split(anom)
    for fetch in fetches:
        fetch.wait()
    target = jnp.concatenate([target_ref[:, i, :] for i in range(6)], 1)
    innov = ((target - preds) / NOISE_STD).astype(BF16)
    state = jnp.concatenate([state_ref[:, i, :] for i in range(8)], 1)
    if mix_hbm:
        state = jnp.dot(mix_ref[...], state, precision=HIGHEST, preferred_element_type=F32)
    par_anom = (state - jnp.mean(state, axis=0, keepdims=True)) * (share / (MEMBERS - 1) ** 0.5)
    lefts = [jnp.concatenate(pair, 1) for pair in zip(lefts_seen, split(par_anom))]
    nothing = jnp.zeros_like(innov)
    rights = [jnp.concatenate(pair, 1) for pair in zip((innov, nothing, nothing), split(-state))]
    lhs = jnp.concatenate(lefts, 0)
    rhs = jnp.concatenate([term for pair in zip(lefts, rights) for term in pair], 0)
    terms = lax.dot_general(lhs, rhs, (((1,), (1,)), ((), ())), preferred_element_type=F32)
    terms = terms[0:32] + terms[32:64] + terms[64:96]
    both = terms[:, 0:64] + terms[:, 64:128] + terms[:, 128:192]
    packed = jnp.concatenate([both[0:16], both[16:32]], 1)
    for i in range(32):
        out_ref[i] = packed


def member_sums(preds, slab, *mix):
    return pl.pallas_call(
        sums_kernel,
        out_shape=pltpu.VMEM((32, 16, 128), F32),
        in_specs=[VMEM, ANY] + [ANY for _ in mix],
        out_specs=VMEM,
        scratch_shapes=[
            pltpu.VMEM((32, 6, 128), F32),
            pltpu.VMEM((32, 8, 128), F32),
            pltpu.VMEM((32, 8, 256), F32),
            pltpu.VMEM((32, 32), F32),
            pltpu.SemaphoreType.DMA((3,)),
        ],
        name="member_sums",
    )(in_vmem(preds), slab, *mix)


def solve_block(block, right):
    half = len(block) // 2
    if half == 1:
        (a, b), (c, d) = block
        inverse = 1.0 / (a * d - b * c)
        return [
            [(d * u - b * l) * inverse for u, l in zip(*right)],
            [(a * l - c * u) * inverse for u, l in zip(*right)],
        ]

    def less(rows, factors, others):
        return [
            [x - sum(f * o[j] for f, o in zip(factor, others)) for j, x in enumerate(row)]
            for row, factor in zip(rows, factors)
        ]

    upper, lower = block[:half], block[half:]
    solved = solve_block([row[:half] for row in upper], [row[half:] + r for row, r in zip(upper, right)])
    edge, top = [row[:half] for row in solved], [row[half:] for row in solved]
    left = [row[:half] for row in lower]
    bottom = solve_block(less([row[half:] for row in lower], left, edge), less(right[half:], left, top))
    return less(top, edge, bottom) + bottom


def solve_kernel(last, parts_ref, slab_ref, *rest):
    *mix_hbm, given_ref, state_ref, held_ref, mixing_ref, mix_ref, sem, mix_sem = rest
    z, core = lax.axis_index("z"), lax.axis_index("core")
    if mix_hbm:
        mix_fetch = pltpu.make_async_copy(mix_hbm[0], mix_ref, mix_sem)
        mix_fetch.start()
    if last:
        wanted = slab_ref.at[:, pl.ds(NOTES, ROWS), :]
    else:
        wanted = slab_ref.at[:, pl.ds(NOTES, ROWS), pl.ds(pl.multiple_of(core * 256, 256), 256)]
    fetch = pltpu.make_async_copy(wanted, held_ref, sem)
    fetch.start()
    both = parts_ref[0]
    for i in range(1, 16):
        both = both + parts_ref[i]
    gram = jnp.concatenate([both[:, 0:32], both[:, 64:96]], 0)
    cross = jnp.concatenate([both[:, 32:64], both[:, 96:128]], 0)
    r = lax.broadcasted_iota(jnp.int32, (32, 32), 0)
    s = lax.broadcasted_iota(jnp.int32, (32, 32), 1)
    eye = (r == s).astype(F32)
    trace = jnp.sum(jnp.sum(gram * eye, axis=1, keepdims=True), axis=0, keepdims=True)
    system = gram + (RIDGE_SHARE / MEMBERS) * trace * eye
    table = jnp.concatenate([system, cross], 1)
    line = lax.broadcasted_iota(jnp.int32, (32, 64), 0)
    step = 2 if last else 4
    for k in range(0, 32, step):
        columns = [jnp.broadcast_to(table[:, k + j : k + j + 1], (32, 64)) for j in range(step)]
        block = [[column[k + i : k + i + 1] for column in columns] for i in range(step)]
        rows = solve_block(block, [[table[k + i : k + i + 1, :]] for i in range(step)])
        for column, (row,) in zip(columns, rows):
            table = table - column * row
        for i, (row,) in enumerate(rows):
            table = jnp.where(line == k + i, row, table)
    coefficients = table[:, 32:64]
    turned = lax.dot_general(
        coefficients, eye, (((0,), (0,)), ((), ())), precision=HIGHEST, preferred_element_type=F32
    )
    centred = turned - jnp.mean(turned, axis=1, keepdims=True)
    mixing = eye + centred / (MEMBERS - 1) ** 0.5
    if mix_hbm:
        mix_fetch.wait()
        mixing = jnp.dot(mixing, mix_ref[...], precision=HIGHEST, preferred_element_type=F32)
    mixing_ref[...] = mixing
    given_ref[...] = coefficients if last else mixing
    count = 2 if last else 4
    rows = mixing_ref[pl.ds(z * 4 + core * 2 if last else z * 4, count), :]
    fetch.wait()
    for i in range(count):
        total = None
        for j in range(MEMBERS):
            part = rows[i : i + 1, j : j + 1] * held_ref[j]
            total = part if total is None else total + part
        if last:
            for row in range(ROWS):
                state_ref[i : i + 1, 512 * row : 512 * row + 512] = total[row : row + 1, :]
        else:
            for y in range(8):
                state_ref[y, i] = total.astype(BF16)


def solve(last, parts, slab, *mix):
    if last:
        outs = jax.ShapeDtypeStruct((32, 32), F32), jax.ShapeDtypeStruct((2, ROWS * 512), F32)
    else:
        outs = jax.ShapeDtypeStruct((32, 32), F32), pltpu.VMEM((8, 4, ROWS, 256), BF16)
    return pl.pallas_call(
        functools.partial(solve_kernel, last),
        out_shape=outs,
        in_specs=[VMEM, ANY] + [ANY for _ in mix],
        out_specs=(VMEM,) * 2,
        scratch_shapes=[
            pltpu.VMEM((MEMBERS, ROWS, 512 if last else 256), F32),
            pltpu.VMEM((32, 32), F32),
            pltpu.VMEM((32, 32), F32),
            pltpu.SemaphoreType.DMA,
            pltpu.SemaphoreType.DMA,
        ],
        name="solve",
    )(in_vmem(parts), slab, *mix)


def exchange(blocks, axes):
    return lax.all_to_all(blocks, axes, 0, 0, tiled=True)


def swap(block):
    return lax.ppermute(block, "core", [(0, 1), (1, 0)])


def local(ensemble, inputs, features, query_index, observed, perturb):
    core = lax.axis_index("core")
    own, keep, give, ext = prepare(
        ensemble, inputs, query_index.reshape(96, 128), observed.reshape(1, -1), perturb
    )
    slab = lax.all_gather(own, ("z", "core"), axis=0, tiled=True)
    taken = swap(give)
    plane = jnp.where(core == 0, jnp.concatenate([keep, taken]), jnp.concatenate([taken, keep]))
    plane = jnp.broadcast_to(plane[None], (8, 4, ROWS, 256))
    ext = lax.all_gather(ext, "x", axis=0, tiled=True)
    mix = []
    for repeat in range(SUBSTEPS):
        half = exchange(plane.reshape(32, ROWS, 256), ("y", "x")).reshape(32 * ROWS, 256)
        half, ext = lax.optimization_barrier((half, ext))
        other = swap(half)
        preds = evaluate(half, other, ext, features)
        preds = exchange(preds, ("z", "x"))
        parts = exchange(member_sums(preds, slab, *mix), ("x", "z"))
        part = jnp.sum(parts, axis=0)
        parts = exchange(jnp.broadcast_to(part[None], (16, 16, 128)), ("core", "y"))
        given, plane = solve(repeat == SUBSTEPS - 1, parts, slab, *mix)
        mix = [given]
    return (plane, given)


def solution(mesh):
    grid = Mesh(mesh.devices.reshape(8, 2, 8, 4), ("z", "core", "y", "x"))
    member, point = ("z", "core"), ("y", "x")
    in_specs = (
        P(member, point),
        P(point, None),
        P(),
        P(point),
        P(point),
        P(member, point),
    )
    out_specs = (P(member, point), P())
    return jax.shard_map(local, mesh=grid, in_specs=in_specs, out_specs=out_specs, check_vma=False)
```

```python
import functools

import jax
import jax.numpy as jnp
from jax import lax
from jax.experimental import pallas as pl
from jax.experimental.pallas import tpu as pltpu
from jax.sharding import Mesh, PartitionSpec as P

SENSORS = 1024
WIDTH = 256
BASIS = 512
FEATS = 256
QOBS = 64
SUBSTEPS = 2
MEMBERS = 32
NOISE_STD = 0.5
RIDGE_SHARE = 0.5
ROWS = 40
NOTES = 32
F32, BF16 = jnp.float32, jnp.bfloat16
HIGHEST = lax.Precision.HIGHEST
VMEM = pl.BlockSpec(memory_space=pltpu.VMEM)
ANY = pl.BlockSpec(memory_space=pl.ANY)


def in_vmem(x):
    return pltpu.with_memory_space_constraint(x, pltpu.VMEM)


def mxu(a, b):
    return jnp.dot(a, b, preferred_element_type=F32)


def prepare_kernel(ensemble_ref, inputs_ref, picks_ref, observed_ref, perturb_ref, own_ref, keep_ref, give_ref, ext_ref):
    core = lax.axis_index("core")
    for i in range(2):
        for e in range(16):
            for part in range(6):
                at = 768 * e + 128 * part
                row, left = 8 * (e // 4) + part, 128 * (e % 4)
                own_ref[i, row : row + 1, left : left + 128] = (
                    observed_ref[0:1, at : at + 128] + perturb_ref[i : i + 1, at : at + 128]
                )
            own_ref[i, 8 * (e // 4) + 6 : 8 * (e // 4) + 8, 128 * (e % 4) : 128 * (e % 4) + 128] = jnp.zeros((2, 128), F32)
        for row in range(ROWS):
            own_ref[i, NOTES + row : NOTES + row + 1, :] = ensemble_ref[i : i + 1, 512 * row : 512 * row + 512]
        keep_ref[i] = own_ref[i, NOTES:, pl.ds(pl.multiple_of(core * 256, 256), 256)].astype(BF16)
        give_ref[i] = own_ref[i, NOTES:, pl.ds(pl.multiple_of((1 - core) * 256, 256), 256)].astype(BF16)
    ext_ref[:, :SENSORS] = inputs_ref[pl.ds(pl.multiple_of(core * 96, 32), 96), :]
    picks = picks_ref[pl.ds(pl.multiple_of(core * 48, 16), 48), :]
    ext_ref[:48, SENSORS:] = picks.astype(F32).astype(BF16)
    ext_ref[48:, SENSORS:] = jnp.zeros((48, 128), BF16)


def prepare(ensemble, inputs, picks, observed, perturb):
    return pl.pallas_call(
        prepare_kernel,
        out_shape=(
            jax.ShapeDtypeStruct((2, NOTES + ROWS, 512), F32),
            pltpu.VMEM((2, ROWS, 256), BF16),
            pltpu.VMEM((2, ROWS, 256), BF16),
            pltpu.VMEM((96, SENSORS + 128), BF16),
        ),
        in_specs=[VMEM] * 5,
        out_specs=(VMEM,) * 4,
        name="prepare",
    )(ensemble, inputs, picks, observed, perturb)


def evaluate_kernel(
    own_blocks, other_blocks, x_ref, features_hbm, out_ref, whole_ref, chosen_ref, features_ref, own_ref, other_ref, sem
):
    fetch = pltpu.make_async_copy(features_hbm, features_ref, sem)
    fetch.start()
    for blocks, rows in ((own_blocks, own_ref), (other_blocks, other_ref)):
        for p in range(0, 32, 2):
            pair = [blocks[(q % 4) * 8 + q // 4] for q in (p, p + 1)]
            rows[ROWS * p : ROWS * p + 2 * ROWS, :] = jnp.concatenate(pair, 0)
    r = lax.broadcasted_iota(jnp.int32, (256, 256), 0)
    s = lax.broadcasted_iota(jnp.int32, (256, 256), 1)
    mix = (s == ((r + lax.axis_index("core")) % 2) * 128 + r // 2).astype(F32).astype(BF16)

    def narrow(start):
        both = jnp.concatenate([own_ref[start : start + 128, :], other_ref[start : start + 128, :]], 0)
        return mxu(mix, both).astype(BF16)

    branch_in, branch_mid, branch_out, trunk_in, trunk_out = 0, 512, 640, 896, 1024
    halves = (own_ref, other_ref)
    total = None
    for i in range(4):
        part = mxu(x_ref[:, 256 * i : 256 * i + 256], narrow(branch_in + 128 * i))
        total = part if total is None else total + part
    hidden = jnp.tanh(total * SENSORS ** (-0.5)).astype(BF16)
    hidden = jnp.tanh(mxu(hidden, narrow(branch_mid)) * WIDTH ** (-0.5)).astype(BF16)
    fetch.wait()
    trunk_hidden = jnp.tanh(mxu(features_ref[...], narrow(trunk_in)) * FEATS ** (-0.5)).astype(BF16)
    trunk = [
        (mxu(trunk_hidden, half[trunk_out : trunk_out + 256, :]) * WIDTH ** (-0.5)).astype(BF16) for half in halves
    ]
    whole = None
    for c, half in enumerate(halves):
        branch = (mxu(hidden, half[branch_out : branch_out + 256, :]) * WIDTH ** (-0.5)).astype(BF16)
        part = lax.dot_general(branch, trunk[c], (((1,), (1,)), ((), ())), preferred_element_type=F32)
        whole = part if whole is None else whole + part
    whole_ref[...] = whole * BASIS ** (-0.5)
    left = lax.broadcasted_iota(jnp.int32, (48, 128), 1) < QOBS
    for x in range(4):
        picks = x_ref[96 * x : 96 * x + 48, SENSORS:].astype(F32).astype(jnp.int32)
        even = whole_ref[pl.ds(96 * x, 48, stride=2), :]
        odd = whole_ref[pl.ds(96 * x + 1, 48, stride=2), :]
        chosen_ref[48 * x : 48 * x + 48, :] = jnp.where(
            left,
            jnp.take_along_axis(even, picks, axis=1, mode="promise_in_bounds"),
            jnp.take_along_axis(odd, picks, axis=1, mode="promise_in_bounds"),
        )
    for x in range(4):
        for z in range(8):
            at = 48 * x + 6 * z
            out_ref[4 * z + x] = chosen_ref[at : at + 6, :].astype(BF16)


def evaluate(own, other, inputs_ext, features):
    return pl.pallas_call(
        evaluate_kernel,
        out_shape=pltpu.VMEM((32, 6, 128), BF16),
        in_specs=[VMEM] * 3 + [ANY],
        out_specs=VMEM,
        scratch_shapes=[
            pltpu.VMEM((384, 128), F32),
            pltpu.VMEM((192, 128), F32),
            pltpu.VMEM((128, FEATS), BF16),
            pltpu.VMEM((32 * ROWS, 256), BF16),
            pltpu.VMEM((32 * ROWS, 256), BF16),
            pltpu.SemaphoreType.DMA,
        ],
        name="evaluate",
    )(in_vmem(own), in_vmem(other), in_vmem(inputs_ext), features)


def split(x):
    high = x.astype(BF16)
    rest = x - high.astype(F32)
    middle = rest.astype(BF16)
    return high, middle, (rest - middle.astype(F32)).astype(BF16)


def sums_kernel(preds_ref, slab_ref, *rest):
    *mix_hbm, out_ref, preds_f32_ref, target_ref, state_ref, mix_ref, sems = rest
    z, core = lax.axis_index("z"), lax.axis_index("core")
    block = core * 8 + z
    place = z * 2 + core
    share = (place < 10).astype(F32)
    place = jnp.minimum(place, 9)
    row = pl.multiple_of(8 * (block // 4), 8)
    column = pl.multiple_of(128 * (block % 4), 128)
    fetches = [
        pltpu.make_async_copy(slab_ref.at[:, pl.ds(row, 8), pl.ds(column, 128)], target_ref, sems.at[0])
    ]
    row = pl.multiple_of(NOTES + 8 * (place // 2), 8)
    column = pl.multiple_of(256 * (place % 2), 256)
    fetches.append(
        pltpu.make_async_copy(slab_ref.at[:, pl.ds(row, 8), pl.ds(column, 256)], state_ref, sems.at[1])
    )
    if mix_hbm:
        fetches.append(pltpu.make_async_copy(mix_hbm[0], mix_ref, sems.at[2]))
    for fetch in fetches:
        fetch.start()
    preds_f32_ref[...] = preds_ref[...].astype(F32)
    preds = jnp.concatenate([preds_f32_ref[:, i, :] for i in range(6)], 1)
    anom = (preds - jnp.mean(preds, axis=0, keepdims=True)) / (NOISE_STD * (MEMBERS - 1) ** 0.5)
    lefts_seen = split(anom)
    for fetch in fetches:
        fetch.wait()
    target = jnp.concatenate([target_ref[:, i, :] for i in range(6)], 1)
    innov = ((target - preds) / NOISE_STD).astype(BF16)
    state = jnp.concatenate([state_ref[:, i, :] for i in range(8)], 1)
    if mix_hbm:
        state = jnp.dot(mix_ref[...], state, precision=HIGHEST, preferred_element_type=F32)
    par_anom = (state - jnp.mean(state, axis=0, keepdims=True)) * (share / (MEMBERS - 1) ** 0.5)
    lefts = [jnp.concatenate(pair, 1) for pair in zip(lefts_seen, split(par_anom))]
    nothing = jnp.zeros_like(innov)
    rights = [jnp.concatenate(pair, 1) for pair in zip((innov, nothing, nothing), split(-state))]
    lhs = jnp.concatenate(lefts, 0)
    rhs = jnp.concatenate([term for pair in zip(lefts, rights) for term in pair], 0)
    terms = lax.dot_general(lhs, rhs, (((1,), (1,)), ((), ())), preferred_element_type=F32)
    terms = terms[0:32] + terms[32:64] + terms[64:96]
    both = terms[:, 0:64] + terms[:, 64:128] + terms[:, 128:192]
    packed = jnp.concatenate([both[0:16], both[16:32]], 1)
    for i in range(32):
        out_ref[i] = packed


def member_sums(preds, slab, *mix):
    return pl.pallas_call(
        sums_kernel,
        out_shape=pltpu.VMEM((32, 16, 128), F32),
        in_specs=[VMEM, ANY] + [ANY for _ in mix],
        out_specs=VMEM,
        scratch_shapes=[
            pltpu.VMEM((32, 6, 128), F32),
            pltpu.VMEM((32, 8, 128), F32),
            pltpu.VMEM((32, 8, 256), F32),
            pltpu.VMEM((32, 32), F32),
            pltpu.SemaphoreType.DMA((3,)),
        ],
        name="member_sums",
    )(in_vmem(preds), slab, *mix)


def solve_block(block, right):
    half = len(block) // 2
    if half == 1:
        (a, b), (c, d) = block
        inverse = 1.0 / (a * d - b * c)
        return [
            [(d * u - b * l) * inverse for u, l in zip(*right)],
            [(a * l - c * u) * inverse for u, l in zip(*right)],
        ]

    def less(rows, factors, others):
        return [
            [x - sum(f * o[j] for f, o in zip(factor, others)) for j, x in enumerate(row)]
            for row, factor in zip(rows, factors)
        ]

    upper, lower = block[:half], block[half:]
    solved = solve_block([row[:half] for row in upper], [row[half:] + r for row, r in zip(upper, right)])
    edge, top = [row[:half] for row in solved], [row[half:] for row in solved]
    left = [row[:half] for row in lower]
    bottom = solve_block(less([row[half:] for row in lower], left, edge), less(right[half:], left, top))
    return less(top, edge, bottom) + bottom


def solve_kernel(last, parts_ref, slab_ref, *rest):
    *mix_hbm, given_ref, state_ref, held_ref, mixing_ref, mix_ref, sem, mix_sem = rest
    z, core = lax.axis_index("z"), lax.axis_index("core")
    if mix_hbm:
        mix_fetch = pltpu.make_async_copy(mix_hbm[0], mix_ref, mix_sem)
        mix_fetch.start()
    if last:
        wanted = slab_ref.at[:, pl.ds(NOTES, ROWS), :]
    else:
        wanted = slab_ref.at[:, pl.ds(NOTES, ROWS), pl.ds(pl.multiple_of(core * 256, 256), 256)]
    fetch = pltpu.make_async_copy(wanted, held_ref, sem)
    fetch.start()
    both = parts_ref[0]
    for i in range(1, 16):
        both = both + parts_ref[i]
    gram = jnp.concatenate([both[:, 0:32], both[:, 64:96]], 0)
    cross = jnp.concatenate([both[:, 32:64], both[:, 96:128]], 0)
    r = lax.broadcasted_iota(jnp.int32, (32, 32), 0)
    s = lax.broadcasted_iota(jnp.int32, (32, 32), 1)
    eye = (r == s).astype(F32)
    trace = jnp.sum(jnp.sum(gram * eye, axis=1, keepdims=True), axis=0, keepdims=True)
    system = gram + (RIDGE_SHARE / MEMBERS) * trace * eye
    table = jnp.concatenate([system, cross], 1)
    line = lax.broadcasted_iota(jnp.int32, (32, 64), 0)
    step = 2 if last else 4
    for k in range(0, 32, step):
        columns = [jnp.broadcast_to(table[:, k + j : k + j + 1], (32, 64)) for j in range(step)]
        block = [[column[k + i : k + i + 1] for column in columns] for i in range(step)]
        rows = solve_block(block, [[table[k + i : k + i + 1, :]] for i in range(step)])
        for column, (row,) in zip(columns, rows):
            table = table - column * row
        for i, (row,) in enumerate(rows):
            table = jnp.where(line == k + i, row, table)
    coefficients = table[:, 32:64]
    turned = lax.dot_general(
        coefficients, eye, (((0,), (0,)), ((), ())), precision=HIGHEST, preferred_element_type=F32
    )
    centred = turned - jnp.mean(turned, axis=1, keepdims=True)
    mixing = eye + centred / (MEMBERS - 1) ** 0.5
    if mix_hbm:
        mix_fetch.wait()
        mixing = jnp.dot(mixing, mix_ref[...], precision=HIGHEST, preferred_element_type=F32)
    mixing_ref[...] = mixing
    given_ref[...] = coefficients if last else mixing
    count = 2 if last else 4
    rows = mixing_ref[pl.ds(z * 4 + core * 2 if last else z * 4, count), :]
    fetch.wait()
    for i in range(count):
        total = None
        for j in range(MEMBERS):
            part = rows[i : i + 1, j : j + 1] * held_ref[j]
            total = part if total is None else total + part
        if last:
            for row in range(ROWS):
                state_ref[i : i + 1, 512 * row : 512 * row + 512] = total[row : row + 1, :]
        else:
            for y in range(8):
                state_ref[8 * i + y] = total.astype(BF16)


def solve(last, parts, slab, *mix):
    if last:
        outs = jax.ShapeDtypeStruct((32, 32), F32), jax.ShapeDtypeStruct((2, ROWS * 512), F32)
    else:
        outs = jax.ShapeDtypeStruct((32, 32), F32), pltpu.VMEM((32, ROWS, 256), BF16)
    return pl.pallas_call(
        functools.partial(solve_kernel, last),
        out_shape=outs,
        in_specs=[VMEM, ANY] + [ANY for _ in mix],
        out_specs=(VMEM,) * 2,
        scratch_shapes=[
            pltpu.VMEM((MEMBERS, ROWS, 512 if last else 256), F32),
            pltpu.VMEM((32, 32), F32),
            pltpu.VMEM((32, 32), F32),
            pltpu.SemaphoreType.DMA,
            pltpu.SemaphoreType.DMA,
        ],
        name="solve",
    )(in_vmem(parts), slab, *mix)


def exchange(blocks, axes):
    return lax.all_to_all(blocks, axes, 0, 0, tiled=True)


def swap(block):
    return lax.ppermute(block, "core", [(0, 1), (1, 0)])


def local(ensemble, inputs, features, query_index, observed, perturb):
    core = lax.axis_index("core")
    own, keep, give, ext = prepare(
        ensemble, inputs, query_index.reshape(96, 128), observed.reshape(1, -1), perturb
    )
    slab = lax.all_gather(own, ("z", "core"), axis=0, tiled=True)
    taken = swap(give)
    plane = jnp.where(core == 0, jnp.concatenate([keep, taken]), jnp.concatenate([taken, keep]))
    plane = jnp.broadcast_to(plane[:, None], (4, 8, ROWS, 256)).reshape(32, ROWS, 256)
    ext = lax.all_gather(ext, "x", axis=0, tiled=True)
    mix = []
    for repeat in range(SUBSTEPS):
        half = exchange(plane, ("x", "y"))
        half, ext = lax.optimization_barrier((half, ext))
        other = swap(half)
        preds = evaluate(half, other, ext, features)
        preds = exchange(preds, ("z", "x"))
        parts = exchange(member_sums(preds, slab, *mix), ("x", "z"))
        part = jnp.sum(parts, axis=0)
        parts = exchange(jnp.broadcast_to(part[None], (16, 16, 128)), ("core", "y"))
        given, plane = solve(repeat == SUBSTEPS - 1, parts, slab, *mix)
        mix = [given]
    return (plane, given)


def solution(mesh):
    grid = Mesh(mesh.devices.reshape(8, 2, 8, 4), ("z", "core", "y", "x"))
    member, point = ("z", "core"), ("y", "x")
    in_specs = (
        P(member, point),
        P(point, None),
        P(),
        P(point),
        P(point),
        P(member, point),
    )
    out_specs = (P(member, point), P())
    return jax.shard_map(local, mesh=grid, in_specs=in_specs, out_specs=out_specs, check_vma=False)
```
